32 devices in a mesh: tm: 8 (over z, y), space: 4 (over x, core).
Axes of the slice: x: 2, y: 2, z: 4, core: 2. Of those that a mesh axis runs over, the one named last changes fastest.
Arguments:
- start_state: float32 [16384], P('space'), may hold values from -6 to 6
- forcing: float32 [64, 16384], P('tm', 'space'), may hold values from -6 to 6
- iterate: float32 [64, 16384], P('tm', 'space'), may hold values from -6 to 6
- blocks: float32 [256, 64, 448], P('space'), may hold values from -1 to 1, as said below
- columns: int32 [256, 7], P('space'), may hold values from 0 to 255, as said below
- kdiag: float32 [16384], P('space'), may hold values from 1.05 to 1.5
Outputs:
- updated: float32 [64, 16384], P('tm', 'space')
The draws below stay inside these ranges and needn't reach their ends.
Inputs may be any that keep to these rules, and one draw needn't show every extreme that they name: columns[b, 0] = b; every entry lies within 4 of b. The absolute values in any row of blocks sum to at most 1.
All inputs are finite; a program needn't handle non-finite values.
Results may differ from the reference program's by a relative error of at most 0.0003.
Values sent between devices are 32-bit elements; how exact they have to be, the bound alone decides.
No kernel may reach another device: no remote copies, remote signals or barrier semaphores. Data moves between devices by JAX's collectives and lax.ppermute only.
A program may use at most 64 MiB of HBM per device.

```python
import jax
import jax.numpy as jnp
from jax import lax

BS = 64
NNZB = 7
GHOST = 4
SWEEPS = 2
NB = 256
ROWS = 16384
NT = 64


def draw_columns(key, part):
    own_rows = lax.iota(jnp.int32, NB)[:, None]
    offsets = jax.random.randint(key, (NB, NNZB - 1), -GHOST, GHOST + 1)
    others = jnp.clip(own_rows + offsets, 0, NB - 1)
    return jnp.concatenate([own_rows, others], axis=1).astype(jnp.int32)


def draw_blocks(key, part):
    shifts = jax.random.randint(jax.random.fold_in(key, 21), (NB, 1, NNZB, 1), 0, BS)
    row_ids = lax.iota(jnp.int32, BS)[None, :, None, None]
    col_ids = lax.iota(jnp.int32, BS)[None, None, None, :]
    hits = jnp.where((row_ids + shifts) % BS == col_ids, 1.0, 0.0).astype(jnp.float32)
    slot_raw = jnp.exp(5.0 * jax.random.uniform(jax.random.fold_in(key, 22), (NB, BS, NNZB, 1), jnp.float32, 0.0, 1.0))
    slot_share = slot_raw / jnp.sum(slot_raw, axis=2, keepdims=True)
    noise = jax.random.uniform(jax.random.fold_in(key, 23), (NB, BS, NNZB, BS), jnp.float32, -1.0, 1.0)
    flips = jax.random.uniform(jax.random.fold_in(key, 24), (NB, BS, NNZB, 1), jnp.float32, 0.0, 1.0)
    signs = jnp.where(flips < 0.5, -1.0, 1.0).astype(jnp.float32)
    totals = jax.random.uniform(jax.random.fold_in(key, 25), (NB, BS, 1, 1), jnp.float32, 0.75, 1.0)
    values = totals * (0.65 * signs * slot_share * hits + 0.35 / (NNZB * BS) * noise)
    return values.reshape(NB, BS, NNZB * BS)


def block_levels(rng, dims, cuts, smallest, high):
    gain, own = 1.0, jax.random.fold_in(rng, 6)
    for axis_at, blocks in cuts:
        heights = jnp.exp(jax.random.uniform(jax.random.fold_in(own, axis_at), (blocks,), jnp.float32, smallest / len(cuts), high / len(cuts)))
        gain = gain * jnp.repeat(heights, dims[axis_at] // blocks).reshape([-1 if axis == axis_at else 1 for axis in range(len(dims))])
    return gain


def gaussian(own_key, dims, scale, bound, split=(), kind=jnp.bfloat16):
    gain = block_levels(own_key, dims, split, -0.22, 0.18) if split else 1.0
    drawn = jax.random.normal(own_key, dims, jnp.float32) * scale * gain
    return jnp.minimum(jnp.maximum(drawn, -bound), bound).astype(kind)


def setup_inputs(seed: int = 0) -> dict:
    splits = jax.random.split(jax.random.key(seed), 7)
    return {
        "start_state": gaussian(splits[0], (ROWS,), 1.0, 6.0, ((0, 4),), jnp.float32),
        "forcing": gaussian(splits[1], (NT, ROWS), 1.0, 6.0, ((0, 8), (1, 4)), jnp.float32),
        "iterate": gaussian(splits[2], (NT, ROWS), 1.0, 6.0, ((0, 8), (1, 4)), jnp.float32),
        "blocks": draw_blocks(jax.random.fold_in(splits[6], 71), 0),
        "columns": draw_columns(jax.random.fold_in(splits[6], 71), 0),
        "kdiag": jnp.clip(1.05 + 0.45000005 * jax.random.uniform(splits[5], (ROWS,), jnp.float32) ** block_levels(splits[5], (ROWS,), ((0, 4),), -0.2, 0.2), 1.05, 1.5),
    }


CORNER_WEIGHT = 0.05


def block_product(blocks, columns, field):
    block_count = blocks.shape[0]
    block_size = blocks.shape[1]

    def one_row(values):
        picked = values.reshape(block_count, block_size)[columns].reshape(block_count, -1)
        return jnp.einsum("bim,bm->bi", blocks, picked, precision=lax.Precision.HIGHEST).reshape(-1)

    return lax.map(one_row, field)


def reference(start_state, forcing, iterate, blocks, columns, kdiag):
    previous = jnp.concatenate([start_state[None], iterate[:-1]], axis=0)
    coupled = block_product(blocks, columns, iterate)
    residual = forcing + previous - iterate - kdiag[None] * iterate - coupled
    steps_all = jnp.arange(NT).astype(jnp.float32)
    scale_up = jnp.power(jnp.float32(CORNER_WEIGHT), steps_all / NT)
    spectrum = jnp.fft.fft(scale_up[:, None] * residual, axis=0)
    spec_re = jnp.real(spectrum)
    spec_im = jnp.imag(spectrum)
    root = CORNER_WEIGHT ** (1.0 / NT)
    theta = 2.0 * jnp.pi * steps_all / NT
    lam_re = 1.0 - root * jnp.cos(theta)
    lam_im = root * jnp.sin(theta)
    diag_re = lam_re[:, None] + kdiag[None]
    diag_im = jnp.broadcast_to(lam_im[:, None], diag_re.shape)
    denom = diag_re * diag_re + diag_im * diag_im

    def divide(num_re, num_im):
        return (num_re * diag_re + num_im * diag_im) / denom, (num_im * diag_re - num_re * diag_im) / denom

    sol_re, sol_im = divide(spec_re, spec_im)
    for sweep_index in range(SWEEPS):
        coupled_both = block_product(blocks, columns, jnp.concatenate([sol_re, sol_im], axis=0))
        sol_re, sol_im = divide(spec_re - coupled_both[:NT], spec_im - coupled_both[NT:])
    back = jnp.real(jnp.fft.ifft(sol_re + 1j * sol_im, axis=0))
    scale_down = jnp.power(jnp.float32(CORNER_WEIGHT), -steps_all / NT)
    return iterate + scale_down[:, None] * back
```

```python
import functools
import math

import jax
import jax.numpy as jnp
import numpy as np
from jax import lax
from jax.experimental import pallas as pl
from jax.experimental.pallas import tpu as pltpu
from jax.sharding import PartitionSpec as P

GHOST = 4
CORNER_WEIGHT = 0.05
AXES = ("tm", "space")
F32 = jnp.float32
BF16 = jnp.bfloat16


def snake(count):
    order = []
    for pair in range(0, count - 1, 2):
        order += [pair, pair + 1] if pair % 4 == 0 else [pair + 1, pair]
    return order + ([count - 1] if count % 2 else [])


def split(value):
    high = value.astype(BF16)
    return high, (value - high.astype(F32)).astype(BF16)


def np_split(value):
    high = value.astype(np.float32).astype(BF16)
    return high, (value - high.astype(np.float64)).astype(np.float32).astype(BF16)


def tables(total, times):
    half = total // 2
    freq = np.arange(half)
    t = np.asarray(times)[:, None]
    angle = 2.0 * math.pi * ((t * freq[None]) % total) / total
    nyquist = np.where(t % 2 == 0, 1.0, -1.0)
    cos, sin = np.cos(angle), np.sin(angle)
    grow = CORNER_WEIGHT ** (t / total)
    forward = np.concatenate([cos, nyquist, -sin[:, 1:]], axis=1) * grow
    twice = np.where(freq == 0, 1.0, 2.0)[None]
    back = np.concatenate([twice * cos, nyquist, -2.0 * sin[:, 1:]], axis=1) / grow / total
    high, low = np_split(forward)
    forward = np.concatenate([high, high, low, low], axis=0)
    high, low = np_split(back)
    back = np.concatenate([high, high, low, low], axis=1)
    root = CORNER_WEIGHT ** (1.0 / total)
    theta = 2.0 * math.pi * freq / total
    lam_re = np.concatenate([1.0 - root * np.cos(theta), [1.0 + root], 1.0 - root * np.cos(theta[1:])])
    lam_im = np.concatenate([root * np.sin(theta), [0.0], -root * np.sin(theta[1:])])
    return forward, back, np.stack([lam_re, lam_im]).astype(np.float32)


def blocks_kernel(sel_ref, own_ref, halo_ref, out_ref):
    take = sel_ref[1, pl.program_id(0)]
    value = jnp.where(take == 1, halo_ref[...], own_ref[...])
    high, low = split(value)
    size = value.shape[1]
    out_ref[:, :size] = high
    out_ref[:, size:] = low


def product(a_ref, row, cols_ref, base, v_ref, size, slots, channels):
    picked = []
    for n in range(slots):
        at = pl.multiple_of((cols_ref[row, n] + base) * size, size)
        picked.append(v_ref[pl.ds(at, size), :])
    picked = jnp.concatenate(picked, axis=0)
    out = jnp.dot(a_ref[row], picked, preferred_element_type=F32)
    out = out[:size] + out[size:]
    return out[:, :channels] + out[:, channels:]


def store_split(ref, at, value):
    high, low = split(value)
    rows, channels = value.shape
    ref[at : at + rows, :channels] = high
    ref[at : at + rows, channels:] = low


def residual_kernel(
    dims, cols_ref, before_ref, a_ref, x_ref, f_ref, left_ref, right_ref, start_ref, kd_ref, out_ref, v_ref, c_ref
):
    size, slots, chunk, total, steps = dims
    rows = chunk * size
    edge = GHOST * size
    store_split(v_ref, 0, left_ref[...].T)
    store_split(v_ref, edge, x_ref[...].T)
    store_split(v_ref, edge + rows, right_ref[...].T)
    for b in range(chunk):
        c_ref[b * size : (b + 1) * size, :] = product(a_ref, b + GHOST, cols_ref, 0, v_ref, size, slots, total)
    coupled = c_ref[...].T
    keep = 1.0 + kd_ref[...]
    for at in range(0, total, steps):
        last = before_ref[at // steps]
        previous = jnp.where(last < 0, start_ref[...], x_ref[pl.ds(jnp.maximum(last, 0), 1), :])
        span = slice(at, at + steps)
        now = x_ref[span, :]
        previous = jnp.concatenate([previous, now[: steps - 1]], axis=0)
        out_ref[span, :] = f_ref[span, :] + previous - keep * now - coupled[span]


def sweeps_kernel(
    dims, cols_ref, a_ref, x_ref, r_ref, left_ref, right_ref, kd_ref, fwd_ref, back_ref, lam_ref, out_ref, s_ref, cr_ref, ci_ref, v0_ref, v1_ref, y_ref
):
    size, slots, chunk, total, _ = dims
    rows = chunk * size
    wide = 2 * GHOST * size
    half = total // 2

    def forward(value):
        high, low = split(value)
        stacked = jnp.concatenate([high, low, high, low], axis=0)
        return lax.dot_general(stacked, fwd_ref[...], (((0,), (0,)), ((), ())), preferred_element_type=F32)

    s_ref[0:wide, :] = forward(left_ref[...])
    s_ref[wide : wide + rows, :] = forward(r_ref[...])
    s_ref[wide + rows :, :] = forward(right_ref[...])
    kd = jnp.broadcast_to(kd_ref[...], (total, kd_ref.shape[1])).T
    diag = kd + lam_ref[0:1, :]
    imag = lam_ref[1:2, :]
    inverse = 1.0 / (diag * diag + imag * imag)
    cr_ref[...] = diag * inverse
    ci_ref[...] = imag * inverse

    def divide(value, at):
        swapped = jnp.concatenate([value[:, half:], value[:, :half]], axis=1)
        span = slice(at, at + value.shape[0])
        return value * cr_ref[span, :] + swapped * ci_ref[span, :]

    store_split(v0_ref, 0, divide(s_ref[...], 0))
    for b in range(chunk + 2 * GHOST):
        at = (b + GHOST) * size
        coupled = product(a_ref, b, cols_ref, GHOST, v0_ref, size, slots, total)
        store_split(v1_ref, b * size, divide(s_ref[at : at + size, :] - coupled, at))
    for b in range(chunk):
        at = (b + 2 * GHOST) * size
        coupled = product(a_ref, b + GHOST, cols_ref, 0, v1_ref, size, slots, total)
        high, low = split(divide(s_ref[at : at + size, :] - coupled, at))
        y_ref[b * size : (b + 1) * size, :] = jnp.concatenate([high, low, high, low], axis=1)
    change = lax.dot_general(back_ref[...], y_ref[...], (((1,), (1,)), ((), ())), preferred_element_type=F32)
    out_ref[...] = x_ref[...] + change


def vmem(count):
    return [pl.BlockSpec(memory_space=pltpu.VMEM)] * count


def smem(count):
    return [pl.BlockSpec(memory_space=pltpu.SMEM)] * count


PARAMS = pltpu.CompilerParams(vmem_limit_bytes=48 * 1024 * 1024)


def local(start_state, forcing, iterate, blocks, columns, kdiag):
    steps, rows_dev = iterate.shape
    block_rows, size, width = blocks.shape
    slots = width // size
    n_tm, n_space = lax.axis_size("tm"), lax.axis_size("space")
    total = steps * n_tm
    chunk = block_rows // n_tm
    rows = chunk * size
    edge = GHOST * size
    wide = 2 * edge
    dims = (size, slots, chunk, total, steps)
    order = snake(n_tm)
    place = [order.index(t) for t in range(n_tm)]

    tm_index, space_index = lax.axis_index("tm"), lax.axis_index("space")
    flipped = space_index % 2 == 1
    spot = jnp.asarray(place, jnp.int32)[tm_index]
    spot = jnp.where(flipped, n_tm - 1 - spot, spot)
    even = (space_index * n_tm + spot) % 2 == 0

    groups, ring = [], []
    for s in range(n_space):
        members = [t * n_space + s for t in (order if s % 2 == 0 else order[::-1])]
        groups.append(tuple(members))
        ring += members
    groups = tuple(groups)
    count = len(ring)

    def deal(value):
        return lax.all_to_all(value, AXES, 0, 0, axis_index_groups=groups, tiled=True)

    def ring_pairs(first):
        pairs = []
        for i in range(first, count - 1, 2):
            pairs += [(ring[i], ring[i + 1]), (ring[i + 1], ring[i])]
        return pairs

    def turned(value, crossed):
        other = value.reshape(n_tm, steps, -1)[::-1].reshape(value.shape)
        return jnp.where(crossed, other, value)

    def neighbours(value, extent):
        if extent <= rows:
            low, high = value[:, :extent], value[:, rows - extent :]
            from_a = lax.ppermute(jnp.where(even, high, low), AXES, ring_pairs(0))
            from_b = lax.ppermute(jnp.where(even, low, high), AXES, ring_pairs(1))
            left, right = jnp.where(even, from_b, from_a), jnp.where(even, from_a, from_b)
            return turned(left, spot == 0), turned(right, spot == n_tm - 1)
        left, right = [], []
        for hop in range(1, extent // rows + 1):
            up = [(ring[i], ring[i + hop]) for i in range(count - hop)]
            left.insert(0, turned(lax.ppermute(value, AXES, up), spot < hop))
            right.append(turned(lax.ppermute(value, AXES, [(j, i) for i, j in up]), spot >= n_tm - hop))
        return jnp.concatenate(left, axis=1), jnp.concatenate(right, axis=1)

    both = jnp.stack([v.reshape(steps, n_tm, rows).transpose(1, 0, 2) for v in (iterate, forcing)], axis=1)
    dealt = deal(both)
    x = dealt[:, 0].reshape(total, rows)
    f = dealt[:, 1].reshape(total, rows)
    times = [[t * steps + j for t in members for j in range(steps)] for members in (order, order[::-1])]
    made = [tables(total, at) for at in times]
    fwd = jnp.where(flipped, made[1][0], made[0][0])
    back = jnp.where(flipped, made[1][1], made[0][1])
    lam = jnp.asarray(made[0][2])
    lasts = [[at.index(at[j] - 1) if at[j] else -1 for j in range(0, total, steps)] for at in times]
    lasts = jnp.where(flipped, jnp.asarray(lasts[1], jnp.int32), jnp.asarray(lasts[0], jnp.int32))

    def packed(at_blocks, at_columns, at_kdiag):
        return jnp.concatenate(
            [at_blocks.reshape(edge, width), jnp.pad(at_columns.astype(F32).reshape(1, -1), ((0, 0), (0, width - GHOST * slots)))]
            + [jnp.pad(at_kdiag.reshape(2, edge), ((0, 0), (0, width - edge)))], axis=0
        )

    low = packed(blocks[:GHOST], columns[:GHOST], kdiag[:wide])
    high = packed(blocks[-GHOST:], columns[-GHOST:], kdiag[-wide:])
    if chunk >= 2 * GHOST and n_tm > 1:
        pairs = []
        for s in range(n_space - 1):
            i, j = ring[(s + 1) * n_tm - 1], ring[(s + 1) * n_tm]
            pairs += [(i, j), (j, i)]
        before = after = lax.ppermute(jnp.where(spot == 0, low, high), AXES, pairs)
    else:
        up = [(s, s + 1) for s in range(n_space - 1)]
        before = lax.ppermute(high, "space", up)
        after = lax.ppermute(low, "space", [(j, i) for i, j in up])

    def unpacked(value):
        return (
            value[:edge].reshape(GHOST, size, width),
            value[edge, : GHOST * slots].reshape(GHOST, slots).astype(jnp.int32),
            value[edge + 1 :, :edge].reshape(-1),
        )

    blocks_before, columns_before, kdiag_before = unpacked(before)
    blocks_after, columns_after, kdiag_after = unpacked(after)
    origin = spot * chunk
    columns_all = jnp.concatenate([columns_before, columns, columns_after], axis=0)
    cols = lax.dynamic_slice_in_dim(columns_all, origin, chunk + 2 * GHOST, 0)
    cols = jnp.clip(cols - (space_index * block_rows + origin - GHOST), -GHOST, chunk + 3 * GHOST - 1)
    kdiag_all = jnp.concatenate([kdiag_before, kdiag, kdiag_after])
    kd = lax.dynamic_slice_in_dim(kdiag_all, origin * size, rows + 2 * wide, 0)[None]
    kd_own = lax.dynamic_slice_in_dim(kdiag, origin * size, rows, 0)[None]
    start = lax.dynamic_slice_in_dim(start_state, origin * size, rows, 0)[None]

    unit = math.gcd(chunk, GHOST)
    pieces = (chunk + 2 * GHOST) // unit
    at = (origin - GHOST) // unit + jnp.arange(pieces)
    own_units, halo_units = block_rows // unit, GHOST // unit
    outside = (at < 0) | (at >= own_units)
    halo_at = jnp.where(at < 0, at + halo_units, at - own_units + halo_units)
    if before is after:
        halo = blocks_before
        halo_at = jnp.where(at < 0, halo_at, halo_at - halo_units)
        halo_last = halo_units - 1
    else:
        halo = jnp.concatenate([blocks_before, blocks_after], axis=0)
        halo_last = 2 * halo_units - 1
    sel = jnp.stack([jnp.clip(at, 0, own_units - 1), outside, jnp.clip(halo_at, 0, halo_last)]).astype(jnp.int32)
    a = pl.pallas_call(
        blocks_kernel,
        grid_spec=pltpu.PrefetchScalarGridSpec(
            num_scalar_prefetch=1,
            grid=(pieces,),
            in_specs=[
                pl.BlockSpec((unit, size, width), lambda i, sel: (sel[0, i], 0, 0)),
                pl.BlockSpec((unit, size, width), lambda i, sel: (sel[2, i], 0, 0)),
            ],
            out_specs=pl.BlockSpec((unit, 2 * size, width), lambda i, sel: (i, 0, 0)),
        ),
        out_shape=jax.ShapeDtypeStruct((chunk + 2 * GHOST, 2 * size, width), BF16),
        compiler_params=PARAMS,
        name="split_blocks",
    )(sel, blocks, halo)

    x_left, x_right = neighbours(x, edge)
    residual = pl.pallas_call(
        functools.partial(residual_kernel, dims),
        in_specs=smem(2) + vmem(7),
        out_specs=vmem(1)[0],
        out_shape=jax.ShapeDtypeStruct((total, rows), F32),
        scratch_shapes=[pltpu.VMEM((rows + 2 * edge, 2 * total), BF16), pltpu.VMEM((rows, total), F32)],
        compiler_params=PARAMS,
        name="residual",
    )(cols, lasts, a, x, f, x_left, x_right, start, kd_own)

    left, right = neighbours(residual, wide)
    span = rows + 2 * wide
    result = pl.pallas_call(
        functools.partial(sweeps_kernel, dims),
        in_specs=smem(1) + vmem(9),
        out_specs=vmem(1)[0],
        out_shape=jax.ShapeDtypeStruct((total, rows), F32),
        scratch_shapes=[pltpu.VMEM((span, total), F32)] * 3
        + [
            pltpu.VMEM((span, 2 * total), BF16),
            pltpu.VMEM((span - wide, 2 * total), BF16),
            pltpu.VMEM((rows, 4 * total), BF16),
        ],
        compiler_params=PARAMS,
        name="sweeps",
    )(cols, a, x, residual, left, right, kd, fwd, back, lam)

    returned = deal(result.reshape(n_tm, steps, rows))
    return returned.transpose(1, 0, 2).reshape(steps, rows_dev)


def solution(mesh):
    placed = (
        P("space"),
        P("tm", "space"),
        P("tm", "space"),
        P("space", None, None),
        P("space", None),
        P("space"),
    )
    return jax.shard_map(local, mesh=mesh, in_specs=placed, out_specs=P("tm", "space"), check_vma=False)
```

```python
import functools
import math

import jax
import jax.numpy as jnp
import numpy as np
from jax import lax
from jax.experimental import pallas as pl
from jax.experimental.pallas import tpu as pltpu
from jax.sharding import PartitionSpec as P

GHOST = 4
CORNER_WEIGHT = 0.05
AXES = ("tm", "space")
F32 = jnp.float32
BF16 = jnp.bfloat16


def there_and_back(count):
    return list(range(0, count, 2)) + list(range(count - 1 - count % 2, 0, -2))


def split(value):
    high = value.astype(BF16)
    return high, (value - high.astype(F32)).astype(BF16)


def np_split(value):
    high = value.astype(np.float32).astype(BF16)
    return high, (value - high.astype(np.float64)).astype(np.float32).astype(BF16)


def tables(total, times):
    half = total // 2
    freq = np.arange(half)
    t = np.asarray(times)[:, None]
    angle = 2.0 * math.pi * ((t * freq[None]) % total) / total
    nyquist = np.where(t % 2 == 0, 1.0, -1.0)
    cos, sin = np.cos(angle), np.sin(angle)
    grow = CORNER_WEIGHT ** (t / total)
    forward = np.concatenate([cos, nyquist, -sin[:, 1:]], axis=1) * grow
    twice = np.where(freq == 0, 1.0, 2.0)[None]
    back = np.concatenate([twice * cos, nyquist, -2.0 * sin[:, 1:]], axis=1) / grow / total
    high, low = np_split(forward)
    forward = np.concatenate([high, high, low, low], axis=0)
    high, low = np_split(back)
    back = np.concatenate([high, high, low, low], axis=1)
    root = CORNER_WEIGHT ** (1.0 / total)
    theta = 2.0 * math.pi * freq / total
    lam_re = np.concatenate([1.0 - root * np.cos(theta), [1.0 + root], 1.0 - root * np.cos(theta[1:])])
    lam_im = np.concatenate([root * np.sin(theta), [0.0], -root * np.sin(theta[1:])])
    return forward, back, np.stack([lam_re, lam_im]).astype(np.float32)


def deal_kernel(x_ref, f_ref, out_ref):
    peers, _, _, rows = out_ref.shape
    for p in range(peers):
        out_ref[p, 0] = x_ref[:, p * rows : (p + 1) * rows]
        out_ref[p, 1] = f_ref[:, p * rows : (p + 1) * rows]


def blocks_kernel(where_ref, cols_ref, blocks_ref, own_ref, near_ref, *rest):
    *edge_ref, buffer, sems = rest
    count, size, width = buffer.shape
    chunk = count - 2 * GHOST
    slots = width // size
    block_rows = blocks_ref.shape[0]
    spot = where_ref[0]
    rows = list(range(GHOST, GHOST + chunk)) + list(range(GHOST)) + list(range(GHOST + chunk, count))
    copies = {}
    for b in rows:
        row = jnp.clip(spot * chunk + b - GHOST, 0, block_rows - 1)
        copies[b] = pltpu.make_async_copy(blocks_ref.at[row], buffer.at[b], sems.at[b])
        copies[b].start()
    for b in rows:
        copies[b].wait()
        high, low = split(buffer[b])
        if GHOST <= b < GHOST + chunk:
            ref, at = own_ref, b - GHOST
        else:
            ref, at = near_ref, b if b < GHOST else b - chunk
        ref[at, :size] = high
        ref[at, size:] = low
    if edge_ref:
        ref = edge_ref[0]
        lane = lax.broadcasted_iota(jnp.int32, (8, width), 1)
        found = jnp.zeros((8, width), jnp.int32)
        for b in range(GHOST):
            inner = jnp.where(spot == 0, buffer[GHOST + b], buffer[chunk + b])
            ref[b * size : (b + 1) * size, :] = inner
            row = jnp.where(spot == 0, b, block_rows - GHOST + b)
            for n in range(slots):
                found = jnp.where(lane == n * GHOST + b, cols_ref[n, row], found)
        ref[GHOST * size :, :] = found.astype(F32)


def patch_kernel(where_ref, old_ref, halo_ref, out_ref):
    size = out_ref.shape[1] // 2
    spot, first, last = where_ref[0], where_ref[3], where_ref[4]

    def put(at, row):
        high, low = split(halo_ref[row * size : (row + 1) * size, :])
        out_ref[at, :size] = high
        out_ref[at, size:] = low

    @pl.when(spot == first)
    def _():
        for b in range(GHOST):
            put(b, b)

    @pl.when(spot == last)
    def _():
        for b in range(GHOST):
            put(GHOST + b, b)


def near_blocks_kernel(sel_ref, own_ref, halo_ref, out_ref):
    take = sel_ref[1, pl.program_id(0)]
    value = jnp.where(take == 1, halo_ref[...], own_ref[...])
    high, low = split(value)
    size = value.shape[1]
    out_ref[:, :size] = high
    out_ref[:, size:] = low


def product(a, at, v_ref, size):
    picked = jnp.concatenate([v_ref[pl.ds(pl.multiple_of(row, size), size), :] for row in at], axis=0)
    out = jnp.dot(a, picked, preferred_element_type=F32)
    out = out[:size] + out[size:]
    channels = out.shape[1] // 2
    return out[:, :channels] + out[:, channels:]


def store_split(ref, at, value):
    high, low = split(value)
    rows, channels = value.shape
    ref[at : at + rows, :channels] = high
    ref[at : at + rows, channels:] = low


def halo(ref, extent, spot, after, dims):
    size, slots, chunk, total, steps = dims
    count = total // steps
    width = min(extent, chunk * size)
    pieces = extent // width
    parts = []
    for p in range(pieces):
        crossed = spot >= count - 1 - p if after else spot < pieces - p
        lanes = slice(p * width, (p + 1) * width)
        rows = []
        for j in range(count):
            at = pl.multiple_of(jnp.where(crossed, count - 1 - j, j) * steps, steps)
            rows.append(ref[pl.ds(at, steps), lanes])
        parts.append(jnp.concatenate(rows, axis=0))
    return parts[0] if pieces == 1 else jnp.concatenate(parts, axis=1)


def row_of(ref, spot, rows):
    tall = rows // 128
    part = ref[pl.ds(spot * tall, tall), :]
    return jnp.concatenate([part[i : i + 1] for i in range(tall)], axis=1)


def residual_kernel(
    dims, lasts, where_ref, cols_ref, a_ref, x_ref, f_ref, left_ref, right_ref, start_ref, kd_ref, out_ref, v_ref, c_ref
):
    size, slots, chunk, total, steps = dims
    rows = chunk * size
    edge = GHOST * size
    spot, flip, base = where_ref[0], where_ref[1], where_ref[2]
    store_split(v_ref, 0, halo(left_ref, edge, spot, False, dims).T)
    store_split(v_ref, edge, x_ref[...].T)
    store_split(v_ref, edge + rows, halo(right_ref, edge, spot, True, dims).T)
    for b in range(chunk):
        at = [(cols_ref[n, spot * chunk + b] - base + GHOST) * size for n in range(slots)]
        c_ref[b * size : (b + 1) * size, :] = product(a_ref[b], at, v_ref, size)
    coupled = c_ref[...].T
    kd = row_of(kd_ref, spot, rows)
    start = row_of(start_ref, spot, rows)
    for j, at in enumerate(range(0, total, steps)):
        last = jnp.where(flip == 1, lasts[1][j], lasts[0][j])
        previous = jnp.where(last < 0, start, x_ref[pl.ds(jnp.maximum(last, 0), 1), :])
        span = slice(at, at + steps)
        now = x_ref[span, :]
        previous = jnp.concatenate([previous, now[: steps - 1]], axis=0)
        out_ref[span, :] = f_ref[span, :] + previous - (1.0 + kd) * now - coupled[span]
    out_ref[total:, :] = jnp.broadcast_to(kd, (8, rows))


def sweeps_kernel(
    dims, where_ref, cols_ref, near_ref, a_ref, an_ref, x_ref, r_ref, left_ref, right_ref, fwd_ref, back_ref, lam_ref, out_ref,
    s_ref, cr_ref, ci_ref, v0_ref, v1_ref, y_ref,
):
    size, slots, chunk, total, _ = dims
    rows = chunk * size
    wide = 2 * GHOST * size
    half = total // 2
    spot, flip, base = where_ref[0], where_ref[1], where_ref[2]
    block_rows = cols_ref.shape[1]

    def forward(value):
        high, low = split(value)
        stacked = jnp.concatenate([high, low, high, low], axis=0)
        return lax.dot_general(stacked, fwd_ref[flip], (((0,), (0,)), ((), ())), preferred_element_type=F32)

    s_ref[0:wide, :] = forward(halo(left_ref, wide, spot, False, dims))
    s_ref[wide : wide + rows, :] = forward(r_ref[:total])
    s_ref[wide + rows :, :] = forward(halo(right_ref, wide, spot, True, dims))
    kd = jnp.concatenate([ref[total : total + 1] for ref in (left_ref, r_ref, right_ref)], axis=1)
    kd = jnp.broadcast_to(kd, (total, kd.shape[1])).T
    diag = kd + lam_ref[0:1, :]
    imag = lam_ref[1:2, :]
    inverse = 1.0 / (diag * diag + imag * imag)
    cr_ref[...] = diag * inverse
    ci_ref[...] = imag * inverse

    def divide(value, at):
        swapped = jnp.concatenate([value[:, half:], value[:, :half]], axis=1)
        span = slice(at, at + value.shape[0])
        return value * cr_ref[span, :] + swapped * ci_ref[span, :]

    def column(n, b):
        row = spot * chunk + b
        found = cols_ref[n, jnp.clip(row, 0, block_rows - 1)]
        if b < 0:
            found = jnp.where(row < 0, near_ref[n, jnp.maximum(row + GHOST, 0)], found)
        if b >= chunk:
            found = jnp.where(row >= block_rows, near_ref[n, GHOST + jnp.maximum(row - block_rows, 0)], found)
        return jnp.clip(found - base, -2 * GHOST, chunk + 2 * GHOST - 1)

    store_split(v0_ref, 0, divide(s_ref[...], 0))
    for b in range(-GHOST, chunk + GHOST):
        at = (b + 2 * GHOST) * size
        a = a_ref[b] if 0 <= b < chunk else an_ref[b + GHOST if b < 0 else b - chunk + GHOST]
        coupled = product(a, [(column(n, b) + 2 * GHOST) * size for n in range(slots)], v0_ref, size)
        store_split(v1_ref, at - GHOST * size, divide(s_ref[at : at + size, :] - coupled, at))
    for b in range(chunk):
        at = (b + 2 * GHOST) * size
        coupled = product(a_ref[b], [(column(n, b) + GHOST) * size for n in range(slots)], v1_ref, size)
        high, low = split(divide(s_ref[at : at + size, :] - coupled, at))
        y_ref[b * size : (b + 1) * size, :] = jnp.concatenate([high, low, high, low], axis=1)
    change = lax.dot_general(back_ref[flip], y_ref[...], (((1,), (1,)), ((), ())), preferred_element_type=F32)
    out_ref[...] = x_ref[...] + change


def vmem(count):
    return [pl.BlockSpec(memory_space=pltpu.VMEM)] * count


def smem(count):
    return [pl.BlockSpec(memory_space=pltpu.SMEM)] * count


PARAMS = pltpu.CompilerParams(vmem_limit_bytes=48 * 1024 * 1024)


def local(start_state, forcing, iterate, blocks, columns, kdiag):
    steps, rows_dev = iterate.shape
    block_rows, size, width = blocks.shape
    slots = width // size
    n_tm, n_space = lax.axis_size("tm"), lax.axis_size("space")
    total = steps * n_tm
    chunk = block_rows // n_tm
    rows = chunk * size
    edge = GHOST * size
    wide = 2 * edge
    dims = (size, slots, chunk, total, steps)
    order = there_and_back(n_tm)

    tm_index, space_index = lax.axis_index("tm"), lax.axis_index("space")
    flipped = space_index % 2 == 1
    spot = jnp.where(tm_index % 2 == 0, tm_index // 2, n_tm - 1 - tm_index // 2)
    spot = jnp.where(flipped, n_tm - 1 - spot, spot)
    even = (space_index * n_tm + spot) % 2 == 0

    groups, ring = [], []
    for s in range(n_space):
        members = [t * n_space + s for t in (order if s % 2 == 0 else order[::-1])]
        groups.append(tuple(members))
        ring += members
    groups = tuple(groups)
    count = len(ring)

    def deal(value):
        return lax.all_to_all(value, AXES, 0, 0, axis_index_groups=groups, tiled=True)

    def ring_pairs(first):
        pairs = []
        for i in range(first, count - 1, 2):
            pairs += [(ring[i], ring[i + 1]), (ring[i + 1], ring[i])]
        return pairs

    def neighbours(value, extent):
        if extent <= rows:
            low, high = value[:, :extent], value[:, rows - extent :]
            from_a = lax.ppermute(jnp.where(even, high, low), AXES, ring_pairs(0))
            from_b = lax.ppermute(jnp.where(even, low, high), AXES, ring_pairs(1))
            return jnp.where(even, from_b, from_a), jnp.where(even, from_a, from_b)
        left, right = [], []
        for hop in range(1, extent // rows + 1):
            up = [(ring[i], ring[i + hop]) for i in range(count - hop)]
            left.insert(0, lax.ppermute(value, AXES, up))
            right.append(lax.ppermute(value, AXES, [(j, i) for i, j in up]))
        return jnp.concatenate(left, axis=1), jnp.concatenate(right, axis=1)

    both = pl.pallas_call(
        deal_kernel,
        in_specs=vmem(2),
        out_specs=vmem(1)[0],
        out_shape=jax.ShapeDtypeStruct((n_tm, 2, steps, rows), F32),
        name="deal",
    )(iterate, forcing)
    dealt = deal(both)
    x = dealt[:, 0].reshape(total, rows)
    f = dealt[:, 1].reshape(total, rows)
    times = [[t * steps + j for t in members for j in range(steps)] for members in (order, order[::-1])]
    made = [tables(total, at) for at in times]
    fwd = np.stack([made[0][0], made[1][0]])
    back = np.stack([made[0][1], made[1][1]])
    lasts = [[at.index(at[j] - 1) if at[j] else -1 for j in range(0, total, steps)] for at in times]
    base = space_index * block_rows + spot * chunk
    scalars = [spot, flipped.astype(jnp.int32), base, jnp.int32(0), jnp.int32(n_tm - 1)]
    where = jnp.stack(scalars).astype(jnp.int32)
    columns = columns.T

    alone = chunk >= 2 * GHOST and n_tm > 1
    out_shape = [jax.ShapeDtypeStruct((n, 2 * size, width), BF16) for n in (chunk, 2 * GHOST)]
    if alone:
        out_shape.append(jax.ShapeDtypeStruct((edge + 8, width), F32))
    a_own, a_near, *outer = pl.pallas_call(
        blocks_kernel,
        in_specs=smem(2) + [pl.BlockSpec(memory_space=pl.ANY)],
        out_specs=vmem(len(out_shape)),
        out_shape=out_shape,
        scratch_shapes=[
            pltpu.VMEM((chunk + 2 * GHOST, size, width), F32),
            pltpu.SemaphoreType.DMA((chunk + 2 * GHOST,)),
        ],
        compiler_params=PARAMS,
        name="blocks",
    )(where, columns, blocks)
    if alone:
        pairs = []
        for s in range(n_space - 1):
            i, j = ring[(s + 1) * n_tm - 1], ring[(s + 1) * n_tm]
            pairs += [(i, j), (j, i)]
        outer = lax.ppermute(outer[0], AXES, pairs)
        columns_halo = outer[edge, : GHOST * slots].reshape(slots, GHOST).astype(jnp.int32)
        columns_halo = jnp.concatenate([columns_halo, columns_halo], axis=1)
        a_near = pl.pallas_call(
            patch_kernel,
            in_specs=smem(1) + vmem(2),
            out_specs=vmem(1)[0],
            out_shape=jax.ShapeDtypeStruct(a_near.shape, BF16),
            input_output_aliases={1: 0},
            compiler_params=PARAMS,
            name="patch",
        )(where, a_near, outer)
    else:
        up = [(s, s + 1) for s in range(n_space - 1)]
        down = [(j, i) for i, j in up]
        blocks_halo = [lax.ppermute(blocks[-GHOST:], "space", up), lax.ppermute(blocks[:GHOST], "space", down)]
        blocks_halo = jnp.concatenate(blocks_halo, axis=0)
        columns_halo = [lax.ppermute(columns[:, -GHOST:], "space", up), lax.ppermute(columns[:, :GHOST], "space", down)]
        columns_halo = jnp.concatenate(columns_halo, axis=1)
        unit = math.gcd(chunk, GHOST)
        units = np.arange(0, GHOST, unit)
        at = jnp.concatenate([spot * chunk - GHOST + units, (spot + 1) * chunk + units]) // unit
        own_units, halo_units = block_rows // unit, GHOST // unit
        halo_at = jnp.where(at < 0, at + halo_units, at - own_units + halo_units)
        outside = (at < 0) | (at >= own_units)
        sel = [jnp.clip(at, 0, own_units - 1), outside, jnp.clip(halo_at, 0, 2 * halo_units - 1)]
        a_near = pl.pallas_call(
            near_blocks_kernel,
            grid_spec=pltpu.PrefetchScalarGridSpec(
                num_scalar_prefetch=1,
                grid=(2 * halo_units,),
                in_specs=[
                    pl.BlockSpec((unit, size, width), lambda i, sel: (sel[0, i], 0, 0)),
                    pl.BlockSpec((unit, size, width), lambda i, sel: (sel[2, i], 0, 0)),
                ],
                out_specs=pl.BlockSpec((unit, 2 * size, width), lambda i, sel: (i, 0, 0)),
            ),
            out_shape=jax.ShapeDtypeStruct((2 * GHOST, 2 * size, width), BF16),
            compiler_params=PARAMS,
            name="near_blocks",
        )(jnp.stack(sel).astype(jnp.int32), blocks, blocks_halo)

    x_left, x_right = neighbours(x, edge)
    residual = pl.pallas_call(
        functools.partial(residual_kernel, dims, lasts),
        in_specs=smem(2) + vmem(7),
        out_specs=vmem(1)[0],
        out_shape=jax.ShapeDtypeStruct((total + 8, rows), F32),
        scratch_shapes=[pltpu.VMEM((rows + 2 * edge, 2 * total), BF16), pltpu.VMEM((rows, total), F32)],
        compiler_params=PARAMS,
        name="residual",
    )(where, columns, a_own, x, f, x_left, x_right, start_state.reshape(-1, 128), kdiag.reshape(-1, 128))

    left, right = neighbours(residual, wide)
    span = rows + 2 * wide
    result = pl.pallas_call(
        functools.partial(sweeps_kernel, dims),
        in_specs=smem(3) + vmem(9),
        out_specs=vmem(1)[0],
        out_shape=jax.ShapeDtypeStruct((total, rows), F32),
        scratch_shapes=[pltpu.VMEM((span, total), F32)] * 3
        + [
            pltpu.VMEM((span, 2 * total), BF16),
            pltpu.VMEM((span - wide, 2 * total), BF16),
            pltpu.VMEM((rows, 4 * total), BF16),
        ],
        compiler_params=PARAMS,
        name="sweeps",
    )(where, columns, columns_halo, a_own, a_near, x, residual, left, right, fwd, back, made[0][2])

    returned = deal(result.reshape(n_tm, steps, rows))
    return returned.transpose(1, 0, 2).reshape(steps, rows_dev)


def solution(mesh):
    placed = (
        P("space"),
        P("tm", "space"),
        P("tm", "space"),
        P("space", None, None),
        P("space", None),
        P("space"),
    )
    return jax.shard_map(local, mesh=mesh, in_specs=placed, out_specs=P("tm", "space"), check_vma=False)
```

```python
import functools
import math

import jax
import jax.numpy as jnp
import numpy as np
from jax import lax
from jax.experimental import pallas as pl
from jax.experimental.pallas import tpu as pltpu
from jax.sharding import PartitionSpec as P

GHOST = 4
CORNER_WEIGHT = 0.05
AXES = ("tm", "space")
F32 = jnp.float32
BF16 = jnp.bfloat16


def there_and_back(count):
    return list(range(0, count, 2)) + list(range(count - 1 - count % 2, 0, -2))


def split(value):
    high = value.astype(BF16)
    return high, (value - high.astype(F32)).astype(BF16)


def np_split(value):
    high = value.astype(np.float32).astype(BF16)
    return high, (value - high.astype(np.float64)).astype(np.float32).astype(BF16)


def tables(total, times):
    half = total // 2
    freq = np.arange(half)
    t = np.asarray(times)[:, None]
    angle = 2.0 * math.pi * ((t * freq[None]) % total) / total
    nyquist = np.where(t % 2 == 0, 1.0, -1.0)
    cos, sin = np.cos(angle), np.sin(angle)
    grow = CORNER_WEIGHT ** (t / total)

    def swapped(value):
        return np.roll(value, half, axis=1)

    forward = np.concatenate([cos, nyquist, -sin[:, 1:]], axis=1) * grow
    high, low = np_split(np.concatenate([forward, swapped(forward)], axis=1))
    forward = np.concatenate([high, low], axis=1)
    twice = np.where(freq == 0, 1.0, 2.0)[None]
    high, low = np_split(np.concatenate([twice * cos, nyquist, -2.0 * sin[:, 1:]], axis=1) / grow / total)
    back = np.concatenate([high, swapped(low)] * 2, axis=1)
    root = CORNER_WEIGHT ** (1.0 / total)
    theta = 2.0 * math.pi * freq / total
    lam_re = np.concatenate([1.0 - root * np.cos(theta), [1.0 + root], 1.0 - root * np.cos(theta[1:])])
    lam_im = np.concatenate([root * np.sin(theta), [0.0], -root * np.sin(theta[1:])])
    lam = np.stack([lam_re, lam_im])
    return np.concatenate([forward] * 2, axis=0), back, np.concatenate([lam, swapped(lam)], axis=1).astype(np.float32)


def deal_kernel(x_ref, f_ref, out_ref):
    peers, _, _, rows = out_ref.shape
    for p in range(peers):
        out_ref[p, 0] = x_ref[:, p * rows : (p + 1) * rows]
        out_ref[p, 1] = f_ref[:, p * rows : (p + 1) * rows]


def blocks_kernel(where_ref, cols_ref, blocks_ref, own_ref, near_ref, *rest):
    *edge_ref, buffer, sems = rest
    count, size, width = buffer.shape
    chunk = count - 2 * GHOST
    slots = width // size
    block_rows = blocks_ref.shape[0]
    spot = where_ref[0]
    rows = list(range(GHOST, GHOST + chunk)) + list(range(GHOST)) + list(range(GHOST + chunk, count))
    copies = {}
    for b in rows:
        row = jnp.clip(spot * chunk + b - GHOST, 0, block_rows - 1)
        copies[b] = pltpu.make_async_copy(blocks_ref.at[row], buffer.at[b], sems.at[b])
        copies[b].start()
    for b in rows:
        copies[b].wait()
        high, low = split(buffer[b])
        if GHOST <= b < GHOST + chunk:
            ref, at = own_ref, b - GHOST
        else:
            ref, at = near_ref, b if b < GHOST else b - chunk
        ref[at, :size] = high
        ref[at, size:] = low
    if edge_ref:
        ref = edge_ref[0]
        lane = lax.broadcasted_iota(jnp.int32, (8, width), 1)
        found = jnp.zeros((8, width), jnp.int32)
        for b in range(GHOST):
            inner = jnp.where(spot == 0, buffer[GHOST + b], buffer[chunk + b])
            ref[b * size : (b + 1) * size, :] = inner
            row = jnp.where(spot == 0, b, block_rows - GHOST + b)
            for n in range(slots):
                found = jnp.where(lane == n * GHOST + b, cols_ref[n, row], found)
        ref[GHOST * size :, :] = found.astype(F32)


def patch_kernel(last, where_ref, old_ref, halo_ref, out_ref):
    size = out_ref.shape[1] // 2
    spot = where_ref[0]

    def put(at, row):
        high, low = split(halo_ref[row * size : (row + 1) * size, :])
        out_ref[at, :size] = high
        out_ref[at, size:] = low

    @pl.when(spot == 0)
    def _():
        for b in range(GHOST):
            put(b, b)

    @pl.when(spot == last)
    def _():
        for b in range(GHOST):
            put(GHOST + b, b)


def near_blocks_kernel(sel_ref, own_ref, halo_ref, out_ref):
    take = sel_ref[1, pl.program_id(0)]
    value = jnp.where(take == 1, halo_ref[...], own_ref[...])
    high, low = split(value)
    size = value.shape[1]
    out_ref[:, :size] = high
    out_ref[:, size:] = low


def product(a, at, v_ref, size):
    picked = jnp.concatenate([v_ref[pl.ds(pl.multiple_of(row, size), size), :] for row in at], axis=0)
    out = jnp.dot(a, picked, preferred_element_type=F32)
    out = out[:size] + out[size:]
    half = out.shape[1] // 2
    return out[:, :half] + out[:, half:]


def store_split(ref, at, value):
    high, low = split(value)
    rows, channels = value.shape
    half = ref.shape[1] // 2
    ref[at : at + rows, :channels] = high
    ref[at : at + rows, half : half + channels] = low


def halo(first_ref, second_ref, take_second, extent, spot, after, dims):
    size, slots, chunk, total, steps = dims
    count = total // steps
    width = min(extent, chunk * size)
    pieces = extent // width
    parts = []
    for p in range(pieces):
        crossed = spot >= count - 1 - p if after else spot < pieces - p
        lanes = slice(p * width, (p + 1) * width)
        rows = []
        for j in range(count):
            at = pl.multiple_of(jnp.where(crossed, count - 1 - j, j) * steps, steps)
            first, second = first_ref[pl.ds(at, steps), lanes], second_ref[pl.ds(at, steps), lanes]
            rows.append(jnp.where(take_second, second, first))
        parts.append(jnp.concatenate(rows, axis=0))
    return parts[0] if pieces == 1 else jnp.concatenate(parts, axis=1)


def row_of(ref, spot, rows):
    tall = rows // 128
    part = ref[pl.ds(spot * tall, tall), :]
    return jnp.concatenate([part[i : i + 1] for i in range(tall)], axis=1)


def residual_kernel(
    dims, lasts, where_ref, cols_ref, a_ref, xf_ref, one_ref, two_ref, start_ref, kd_ref, out_ref, v_ref, c_ref
):
    size, slots, chunk, total, steps = dims
    rows = chunk * size
    edge = GHOST * size
    spot, flip, base, even = where_ref[0], where_ref[1], where_ref[2], where_ref[3] == 1
    store_split(v_ref, 0, halo(one_ref, two_ref, even, edge, spot, False, dims).T)
    store_split(v_ref, edge, xf_ref[:, 0].reshape(total, rows).T)
    store_split(v_ref, edge + rows, halo(two_ref, one_ref, even, edge, spot, True, dims).T)
    for b in range(chunk):
        at = [(cols_ref[n, spot * chunk + b] - base + GHOST) * size for n in range(slots)]
        c_ref[b * size : (b + 1) * size, :] = product(a_ref[b], at, v_ref, size)[:, :total]
    coupled = c_ref[...].T
    kd = row_of(kd_ref, spot, rows)
    start = row_of(start_ref, spot, rows)
    for j in range(total // steps):
        last = jnp.where(flip == 1, lasts[1][j], lasts[0][j])
        previous = jnp.where(last < 0, start, xf_ref[jnp.maximum(last, 0), 0, steps - 1 : steps, :])
        span = slice(j * steps, (j + 1) * steps)
        now = xf_ref[j, 0]
        previous = jnp.concatenate([previous, now[: steps - 1]], axis=0)
        out_ref[span, :] = xf_ref[j, 1] + previous - (1.0 + kd) * now - coupled[span]
    out_ref[total:, :] = jnp.broadcast_to(kd, (8, rows))


def sweeps_kernel(
    dims, where_ref, cols_ref, near_ref, a_ref, an_ref, xf_ref, r_ref, one_ref, two_ref, fwd_ref, back_ref, lam_ref, out_ref,
    s_ref, cr_ref, ci_ref, v0_ref, v1_ref, y_ref,
):
    size, slots, chunk, total, _ = dims
    rows = chunk * size
    wide = 2 * GHOST * size
    spot, flip, base, even = where_ref[0], where_ref[1], where_ref[2], where_ref[4] == 1
    block_rows = cols_ref.shape[1]
    fwd = fwd_ref[flip]

    def forward(at, value):
        high, low = split(value)
        stacked = jnp.concatenate([high, low], axis=0)
        out = lax.dot_general(stacked, fwd, (((0,), (0,)), ((), ())), preferred_element_type=F32)
        s_ref[at : at + value.shape[1], :] = out[:, : 2 * total] + out[:, 2 * total :]

    forward(wide, r_ref[:total])
    forward(0, halo(one_ref, two_ref, even, wide, spot, False, dims))
    forward(wide + rows, halo(two_ref, one_ref, even, wide, spot, True, dims))
    first, second = one_ref[total : total + 1], two_ref[total : total + 1]
    left, right = jnp.where(even, second, first), jnp.where(even, first, second)
    kd = jnp.concatenate([left, r_ref[total : total + 1], right], axis=1)
    kd = jnp.broadcast_to(kd, (2 * total, kd.shape[1])).T
    diag = kd + lam_ref[0:1, :]
    imag = lam_ref[1:2, :]
    inverse = 1.0 / (diag * diag + imag * imag)
    cr_ref[...] = diag * inverse
    ci_ref[...] = imag * inverse

    def divide(value, at):
        span = slice(at, at + value.shape[0])
        return value * cr_ref[span, :] + pltpu.roll(value, total, 1) * ci_ref[span, :]

    def column(n, b):
        row = spot * chunk + b
        found = cols_ref[n, jnp.clip(row, 0, block_rows - 1)]
        if b < 0:
            found = jnp.where(row < 0, near_ref[n, jnp.maximum(row + GHOST, 0)], found)
        if b >= chunk:
            found = jnp.where(row >= block_rows, near_ref[n, GHOST + jnp.maximum(row - block_rows, 0)], found)
        return jnp.clip(found - base, -2 * GHOST, chunk + 2 * GHOST - 1)

    store_split(v0_ref, 0, divide(s_ref[...], 0))
    for b in range(-GHOST, chunk + GHOST):
        at = (b + 2 * GHOST) * size
        a = a_ref[b] if 0 <= b < chunk else an_ref[b + GHOST if b < 0 else b - chunk + GHOST]
        coupled = product(a, [(column(n, b) + 2 * GHOST) * size for n in range(slots)], v0_ref, size)
        store_split(v1_ref, at - GHOST * size, divide(s_ref[at : at + size, :] - coupled, at))
    for b in range(chunk):
        at = (b + 2 * GHOST) * size
        coupled = product(a_ref[b], [(column(n, b) + GHOST) * size for n in range(slots)], v1_ref, size)
        store_split(y_ref, b * size, divide(s_ref[at : at + size, :] - coupled, at))
    change = lax.dot_general(back_ref[flip], y_ref[...], (((1,), (1,)), ((), ())), preferred_element_type=F32)
    out_ref[...] = xf_ref[:, 0].reshape(total, rows) + change


def vmem(count):
    return [pl.BlockSpec(memory_space=pltpu.VMEM)] * count


def smem(count):
    return [pl.BlockSpec(memory_space=pltpu.SMEM)] * count


PARAMS = pltpu.CompilerParams(vmem_limit_bytes=16 * 1024 * 1024)
BLOCKS_PARAMS = pltpu.CompilerParams(vmem_limit_bytes=48 * 1024 * 1024)


def local(start_state, forcing, iterate, blocks, columns, kdiag):
    steps, rows_dev = iterate.shape
    block_rows, size, width = blocks.shape
    slots = width // size
    n_tm, n_space = lax.axis_size("tm"), lax.axis_size("space")
    total = steps * n_tm
    chunk = block_rows // n_tm
    rows = chunk * size
    edge = GHOST * size
    wide = 2 * edge
    dims = (size, slots, chunk, total, steps)
    order = there_and_back(n_tm)

    tm_index, space_index = lax.axis_index("tm"), lax.axis_index("space")
    flipped = space_index % 2 == 1
    spot = jnp.where(tm_index % 2 == 0, tm_index // 2, n_tm - 1 - tm_index // 2)
    spot = jnp.where(flipped, n_tm - 1 - spot, spot)
    even = (space_index * n_tm + spot) % 2 == 0

    groups, ring = [], []
    for s in range(n_space):
        members = [t * n_space + s for t in (order if s % 2 == 0 else order[::-1])]
        groups.append(tuple(members))
        ring += members
    groups = tuple(groups)
    count = len(ring)

    def deal(value):
        return lax.all_to_all(value, AXES, 0, 0, axis_index_groups=groups, tiled=True)

    def ring_pairs(first):
        pairs = []
        for i in range(first, count - 1, 2):
            pairs += [(ring[i], ring[i + 1]), (ring[i + 1], ring[i])]
        return pairs

    def neighbours(value, extent):
        if extent <= rows:
            low, high = value[:, :extent], value[:, rows - extent :]
            from_a = lax.ppermute(jnp.where(even, high, low), AXES, ring_pairs(0))
            from_b = lax.ppermute(jnp.where(even, low, high), AXES, ring_pairs(1))
            return from_a, from_b
        left, right = [], []
        for hop in range(1, extent // rows + 1):
            up = [(ring[i], ring[i + hop]) for i in range(count - hop)]
            left.insert(0, lax.ppermute(value, AXES, up))
            right.append(lax.ppermute(value, AXES, [(j, i) for i, j in up]))
        return jnp.concatenate(left, axis=1), jnp.concatenate(right, axis=1)

    both = pl.pallas_call(
        deal_kernel,
        in_specs=vmem(2),
        out_specs=vmem(1)[0],
        out_shape=jax.ShapeDtypeStruct((n_tm, 2, steps, rows), F32),
        name="deal",
    )(iterate, forcing)
    dealt = deal(both)
    x = dealt[:, 0].reshape(total, rows)
    times = [[t * steps + j for t in members for j in range(steps)] for members in (order, order[::-1])]
    made = [tables(total, at) for at in times]
    fwd = np.stack([made[0][0], made[1][0]])
    back = np.stack([made[0][1], made[1][1]])
    lasts = [[at.index(at[j] - 1) // steps if at[j] else -1 for j in range(0, total, steps)] for at in times]
    base = space_index * block_rows + spot * chunk
    where = jnp.stack([spot, flipped, base] + [even & (extent <= rows) for extent in (edge, wide)]).astype(jnp.int32)
    columns = columns.T

    alone = chunk >= 2 * GHOST and n_tm > 1
    out_shape = [jax.ShapeDtypeStruct((n, 2 * size, width), BF16) for n in (chunk, 2 * GHOST)]
    if alone:
        out_shape.append(jax.ShapeDtypeStruct((edge + 8, width), F32))
    a_own, a_near, *outer = pl.pallas_call(
        blocks_kernel,
        in_specs=smem(2) + [pl.BlockSpec(memory_space=pltpu.HBM)],
        out_specs=vmem(len(out_shape)),
        out_shape=out_shape,
        scratch_shapes=[
            pltpu.VMEM((chunk + 2 * GHOST, size, width), F32),
            pltpu.SemaphoreType.DMA((chunk + 2 * GHOST,)),
        ],
        compiler_params=BLOCKS_PARAMS,
        name="blocks",
    )(where, columns, blocks)
    if alone:
        pairs = []
        for s in range(n_space - 1):
            i, j = ring[(s + 1) * n_tm - 1], ring[(s + 1) * n_tm]
            pairs += [(i, j), (j, i)]
        outer = lax.ppermute(outer[0], AXES, pairs)
        columns_halo = outer[edge, : GHOST * slots].reshape(slots, GHOST).astype(jnp.int32)
        columns_halo = jnp.concatenate([columns_halo, columns_halo], axis=1)
        a_near = pl.pallas_call(
            functools.partial(patch_kernel, n_tm - 1),
            in_specs=smem(1) + vmem(2),
            out_specs=vmem(1)[0],
            out_shape=jax.ShapeDtypeStruct(a_near.shape, BF16),
            input_output_aliases={1: 0},
            compiler_params=PARAMS,
            name="patch",
        )(where, a_near, outer)
    else:
        up = [(s, s + 1) for s in range(n_space - 1)]
        down = [(j, i) for i, j in up]
        blocks_halo = [lax.ppermute(blocks[-GHOST:], "space", up), lax.ppermute(blocks[:GHOST], "space", down)]
        blocks_halo = jnp.concatenate(blocks_halo, axis=0)
        columns_halo = [lax.ppermute(columns[:, -GHOST:], "space", up), lax.ppermute(columns[:, :GHOST], "space", down)]
        columns_halo = jnp.concatenate(columns_halo, axis=1)
        unit = math.gcd(chunk, GHOST)
        units = np.arange(0, GHOST, unit)
        at = jnp.concatenate([spot * chunk - GHOST + units, (spot + 1) * chunk + units]) // unit
        own_units, halo_units = block_rows // unit, GHOST // unit
        halo_at = jnp.where(at < 0, at + halo_units, at - own_units + halo_units)
        outside = (at < 0) | (at >= own_units)
        sel = [jnp.clip(at, 0, own_units - 1), outside, jnp.clip(halo_at, 0, 2 * halo_units - 1)]
        a_near = pl.pallas_call(
            near_blocks_kernel,
            grid_spec=pltpu.PrefetchScalarGridSpec(
                num_scalar_prefetch=1,
                grid=(2 * halo_units,),
                in_specs=[
                    pl.BlockSpec((unit, size, width), lambda i, sel: (sel[0, i], 0, 0)),
                    pl.BlockSpec((unit, size, width), lambda i, sel: (sel[2, i], 0, 0)),
                ],
                out_specs=pl.BlockSpec((unit, 2 * size, width), lambda i, sel: (i, 0, 0)),
            ),
            out_shape=jax.ShapeDtypeStruct((2 * GHOST, 2 * size, width), BF16),
            compiler_params=PARAMS,
            name="near_blocks",
        )(jnp.stack(sel).astype(jnp.int32), blocks, blocks_halo)

    one, two = neighbours(x, edge)
    residual = pl.pallas_call(
        functools.partial(residual_kernel, dims, lasts),
        in_specs=smem(2) + vmem(6),
        out_specs=vmem(1)[0],
        out_shape=jax.ShapeDtypeStruct((total + 8, rows), F32),
        scratch_shapes=[pltpu.VMEM((rows + 2 * edge, 2 * max(total, 128)), BF16), pltpu.VMEM((rows, total), F32)],
        compiler_params=PARAMS,
        name="residual",
    )(where, columns, a_own, dealt, one, two, start_state.reshape(-1, 128), kdiag.reshape(-1, 128))

    one, two = neighbours(residual, wide)
    span = rows + 2 * wide
    result = pl.pallas_call(
        functools.partial(sweeps_kernel, dims),
        in_specs=smem(3) + vmem(9),
        out_specs=vmem(1)[0],
        out_shape=jax.ShapeDtypeStruct((total, rows), F32),
        scratch_shapes=[pltpu.VMEM((span, 2 * total), F32)] * 3
        + [pltpu.VMEM((height, 4 * total), BF16) for height in (span, span - wide, rows)],
        compiler_params=PARAMS,
        name="sweeps",
    )(where, columns, columns_halo, a_own, a_near, dealt, residual, one, two, fwd, back, made[0][2])

    returned = deal(result.reshape(n_tm, steps, rows))
    return returned.transpose(1, 0, 2).reshape(steps, rows_dev)


def solution(mesh):
    placed = (
        P("space"),
        P("tm", "space"),
        P("tm", "space"),
        P("space", None, None),
        P("space", None),
        P("space"),
    )
    return jax.shard_map(local, mesh=mesh, in_specs=placed, out_specs=P("tm", "space"), check_vma=False)
```

```python
import functools
import math

import jax
import jax.numpy as jnp
import numpy as np
from jax import lax
from jax.experimental import pallas as pl
from jax.experimental.pallas import tpu as pltpu
from jax.sharding import PartitionSpec as P

GHOST = 4
CORNER_WEIGHT = 0.05
AXES = ("tm", "space")
F32 = jnp.float32
BF16 = jnp.bfloat16


def there_and_back(count):
    return list(range(0, count, 2)) + list(range(count - 1 - count % 2, 0, -2))


def split(value):
    high = value.astype(BF16)
    return high, (value - high.astype(F32)).astype(BF16)


def np_split(value):
    high = value.astype(np.float32).astype(BF16)
    return high, (value - high.astype(np.float64)).astype(np.float32).astype(BF16)


def tables(total, times):
    half = total // 2
    freq = np.arange(half)
    t = np.asarray(times)[:, None]
    angle = 2.0 * math.pi * ((t * freq[None]) % total) / total
    nyquist = np.where(t % 2 == 0, 1.0, -1.0)
    cos, sin = np.cos(angle), np.sin(angle)
    grow = CORNER_WEIGHT ** (t / total)

    def swapped(value):
        return np.roll(value, half, axis=1)

    forward = np.concatenate([cos, nyquist, -sin[:, 1:]], axis=1) * grow
    high, low = np_split(np.concatenate([forward, swapped(forward)], axis=1))
    forward = np.concatenate([high, low], axis=1)
    twice = np.where(freq == 0, 1.0, 2.0)[None]
    high, low = np_split(np.concatenate([twice * cos, nyquist, -2.0 * sin[:, 1:]], axis=1) / grow / total)
    back = np.concatenate([high, swapped(low)] * 2, axis=1)
    root = CORNER_WEIGHT ** (1.0 / total)
    theta = 2.0 * math.pi * freq / total
    lam_re = np.concatenate([1.0 - root * np.cos(theta), [1.0 + root], 1.0 - root * np.cos(theta[1:])])
    lam_im = np.concatenate([root * np.sin(theta), [0.0], -root * np.sin(theta[1:])])
    lam = np.stack([lam_re, lam_im])
    return np.concatenate([forward] * 2, axis=0), back, np.concatenate([lam, swapped(lam)], axis=1).astype(np.float32)


def place(lower_ref, upper_ref, at, value):
    half = value.shape[1] // 2
    turned = pltpu.roll(value, half, 1)
    low = lax.broadcasted_iota(jnp.int32, value.shape, 1) < half
    for i, (first, second) in enumerate(((value, turned), (turned, value))):
        for ref, part in ((lower_ref, jnp.where(low, first, 0.0)), (upper_ref, jnp.where(low, 0.0, second))):
            ref[at + i] = jnp.concatenate(split(part), axis=0)


def couple(block, at, lower_ref, upper_ref):
    size, width = block.shape
    tiles = [lower_ref[at[n]] + upper_ref[at[n + 1]] for n in range(0, len(at) - 1, 2)]
    if len(at) % 2:
        tiles.append(lower_ref[at[-1]])
    picked = jnp.concatenate(tiles, axis=1)[:, :width]
    out = lax.dot_general(
        picked, jnp.concatenate(split(block), axis=0), (((1,), (1,)), ((), ())), preferred_element_type=F32
    )
    steps = out.shape[0] // 2
    out = out[:steps] + out[steps:]
    return out + pltpu.roll(out, size, 1)


def couple_rows(blocks_ref, origin, cols_ref, base, rows, lower_ref, upper_ref, put):
    slots = cols_ref.shape[0]
    size = blocks_ref.shape[1]
    for b in rows:
        pair = [
            couple(blocks_ref[i - origin], [cols_ref[n, i] - base for n in range(slots)], lower_ref, upper_ref)
            for i in (b, b + 1)
        ]
        low = lax.broadcasted_iota(jnp.int32, pair[0].shape, 1) < size
        put(b // 2, jnp.where(low, pair[0], pair[1]))


def sides_kernel(where_ref, x_ref, blocks_ref, one_ref, two_ref):
    even = where_ref[6] == 1
    extent = one_ref.shape[1]
    low, high = x_ref[:, :extent], x_ref[:, x_ref.shape[1] - extent :]
    one_ref[...] = jnp.where(even, high, low)
    two_ref[...] = jnp.where(even, low, high)


def inner_kernel(where_ref, cols_ref, x_ref, blocks_ref, out_ref, lower_ref, upper_ref):
    block_rows = blocks_ref.shape[0]

    def put(i, value):
        out_ref[:, i * 128 : (i + 1) * 128] = value

    for b in range(0, block_rows, 2):
        place(lower_ref, upper_ref, b, x_ref[:, b * 64 : b * 64 + 128])
    rows = range(GHOST, block_rows - GHOST, 2)
    couple_rows(blocks_ref, 0, cols_ref, where_ref[5], rows, lower_ref, upper_ref, put)


def outer_kernel(
    where_ref, cols_ref, x_ref, f_ref, blocks_ref, inner_ref, one_ref, two_ref, start_ref, kd_ref, out_ref, rim_ref,
    lower_ref, upper_ref, edge_ref,
):
    block_rows = cols_ref.shape[1]
    steps = x_ref.shape[0]
    peers, height, _ = out_ref.shape
    tall = x_ref.shape[1] // peers // 128
    even, opening = where_ref[6] == 1, where_ref[7] == 1
    for i in range(0, GHOST, 2):
        lanes = slice(i * 64, i * 64 + 128)
        first, second = one_ref[:, lanes], two_ref[:, lanes]
        place(lower_ref, upper_ref, i, jnp.where(even, second, first))
        place(lower_ref, upper_ref, GHOST + block_rows + i, jnp.where(even, first, second))
    ends = list(range(0, 2 * GHOST, 2)) + list(range(block_rows - 2 * GHOST, block_rows, 2))
    for b in ends:
        place(lower_ref, upper_ref, GHOST + b, x_ref[:, b * 64 : b * 64 + 128])

    def put(i, value):
        edge_ref[i] = value

    outer = [b for b in ends if b < GHOST or b >= block_rows - GHOST]
    couple_rows(blocks_ref, 0, cols_ref, where_ref[5] - GHOST, outer, lower_ref, upper_ref, put)
    for i in range(x_ref.shape[1] // 128):
        lanes = slice(i * 128, (i + 1) * 128)
        now = x_ref[:, lanes]
        coupled = edge_ref[i] if 2 * i in outer else inner_ref[:, lanes]
        kd = kd_ref[i : i + 1, :]
        before = jnp.where(opening, start_ref[i : i + 1, :], 0.0)
        previous = jnp.concatenate([before, now[: steps - 1]], axis=0)
        p, j = i // tall, i % tall
        out_ref[p, j * steps : (j + 1) * steps, :] = f_ref[:, lanes] + previous - (1.0 + kd) * now - coupled
        out_ref[p, steps * tall + j : steps * tall + j + 1, :] = now[steps - 1 :]
        out_ref[p, (steps + 1) * tall + j : (steps + 1) * tall + j + 1, :] = kd
    used = (steps + 2) * tall
    if used < height:
        out_ref[:, used:, :] = jnp.zeros((peers, height - used, 128), F32)

    lowest = where_ref[0] == 0
    _, size, width = blocks_ref.shape
    slots = width // size
    lane = lax.broadcasted_iota(jnp.int32, (8, width), 1)
    found = jnp.zeros((8, width), jnp.int32)
    for b in range(GHOST):
        last = block_rows - GHOST + b
        rim_ref[b * size : (b + 1) * size, :] = jnp.where(lowest, blocks_ref[b], blocks_ref[last])
        for n in range(slots):
            found = jnp.where(lane == n * GHOST + b, cols_ref[n, jnp.where(lowest, b, last)], found)
    rim_ref[GHOST * size :, :] = found.astype(F32)


def blocks_kernel(where_ref, blocks_ref, rim_ref, own_ref, near_ref, buffer, sems):
    count, size, _ = buffer.shape
    chunk = count - 2 * GHOST
    block_rows = blocks_ref.shape[0]
    spot = where_ref[0]
    rows = list(range(GHOST, GHOST + chunk)) + list(range(GHOST)) + list(range(GHOST + chunk, count))
    copies = {}
    for b in rows:
        row = jnp.clip(spot * chunk + b - GHOST, 0, block_rows - 1)
        copies[b] = pltpu.make_async_copy(blocks_ref.at[row], buffer.at[b], sems.at[b])
        copies[b].start()
    for b in rows:
        copies[b].wait()
        value = buffer[b]
        if GHOST <= b < GHOST + chunk:
            ref, at = own_ref, b - GHOST
        else:
            ref, at = near_ref, b if b < GHOST else b - chunk
            row = spot * chunk + b - GHOST
            if rim_ref.shape[0] > GHOST * size + 8:
                at_rim = jnp.where(row < 0, row + GHOST, GHOST + row - block_rows)
            else:
                at_rim = jnp.where(row < 0, row + GHOST, row - block_rows)
            outside = (row < 0) | (row >= block_rows)
            at_rim = pl.multiple_of(jnp.where(outside, at_rim, 0) * size, size)
            value = jnp.where(outside, rim_ref[pl.ds(at_rim, size), :], value)
        high, low = split(value)
        ref[at, :size] = high
        ref[at, size:] = low


def product(a, at, v_ref, size):
    picked = jnp.concatenate([v_ref[pl.ds(pl.multiple_of(row, size), size), :] for row in at], axis=0)
    out = jnp.dot(a, picked, preferred_element_type=F32)
    out = out[:size] + out[size:]
    half = out.shape[1] // 2
    return out[:, :half] + out[:, half:]


def store_split(ref, at, value):
    high, low = split(value)
    rows, channels = value.shape
    half = ref.shape[1] // 2
    ref[at : at + rows, :channels] = high
    ref[at : at + rows, half : half + channels] = low


def gather_chunk(pick, crossed, flip, lasts, dims):
    size, slots, chunk, total, steps = dims
    tall = chunk * size // 128
    count = total // steps
    parts = []
    for j in range(count):
        last = jnp.where(flip == 1, lasts[1][j], lasts[0][j])
        at = jnp.maximum(last, 0)
        held = pick(jnp.where(crossed, count - 1 - j, j))
        other = pick(jnp.where(crossed, count - 1 - at, at))
        wide = [held[i * steps : (i + 1) * steps] for i in range(tall)]
        before = [other[steps * tall + i : steps * tall + i + 1] for i in range(tall)]
        wide, before = jnp.concatenate(wide, axis=1), jnp.concatenate(before, axis=1)
        opens = lax.broadcasted_iota(jnp.int32, wide.shape, 0) == 0
        parts.append(wide + jnp.where(opens & (last >= 0), before, 0.0))
    kd = jnp.concatenate([held[(steps + 1) * tall + i : (steps + 1) * tall + i + 1] for i in range(tall)], axis=1)
    return jnp.concatenate(parts, axis=0), kd


def sweeps_kernel(
    dims, lasts, where_ref, cols_ref, near_ref, a_ref, an_ref, r_ref, one_ref, two_ref, fwd_ref, back_ref, lam_ref, out_ref,
    s_ref, cr_ref, ci_ref, v0_ref, v1_ref, y_ref,
):
    size, slots, chunk, total, steps = dims
    rows = chunk * size
    wide = 2 * GHOST * size
    spot, flip, base, even = where_ref[0], where_ref[1], where_ref[2], where_ref[3] == 1
    count = total // steps
    block_rows = cols_ref.shape[1]
    fwd = fwd_ref[flip]

    def forward(at, value):
        high, low = split(value)
        stacked = jnp.concatenate([high, low], axis=0)
        out = lax.dot_general(stacked, fwd, (((0,), (0,)), ((), ())), preferred_element_type=F32)
        s_ref[at : at + value.shape[1], :] = out[:, : 2 * total] + out[:, 2 * total :]

    def near(first_ref, second_ref, hop):
        return lambda at: jnp.where(even, second_ref[hop, at], first_ref[hop, at])

    hops = one_ref.shape[0]
    chunks = [(near(one_ref, two_ref, h), spot < hops - h) for h in range(hops)]
    chunks += [(lambda at: r_ref[at], False)]
    chunks += [(near(two_ref, one_ref, h), spot >= count - 1 - h) for h in range(hops)]
    kds = []
    for i, (pick, crossed) in enumerate(chunks):
        residual, kd = gather_chunk(pick, crossed, flip, lasts, dims)
        forward(i * rows, residual)
        kds.append(kd)
    kd = jnp.concatenate(kds, axis=1)
    kd = jnp.broadcast_to(kd, (2 * total, kd.shape[1])).T
    diag = kd + lam_ref[0:1, :]
    imag = lam_ref[1:2, :]
    inverse = 1.0 / (diag * diag + imag * imag)
    cr_ref[...] = diag * inverse
    ci_ref[...] = imag * inverse

    def divide(value, at):
        span = slice(at, at + value.shape[0])
        return value * cr_ref[span, :] + pltpu.roll(value, total, 1) * ci_ref[span, :]

    def column(n, b):
        row = spot * chunk + b
        found = cols_ref[n, jnp.clip(row, 0, block_rows - 1)]
        if b < 0:
            found = jnp.where(row < 0, near_ref[n, jnp.maximum(row + GHOST, 0)], found)
        if b >= chunk:
            found = jnp.where(row >= block_rows, near_ref[n, GHOST + jnp.maximum(row - block_rows, 0)], found)
        return jnp.clip(found - base, -2 * GHOST, chunk + 2 * GHOST - 1)

    store_split(v0_ref, 0, divide(s_ref[...], 0))
    for b in range(-GHOST, chunk + GHOST):
        at = (b + 2 * GHOST) * size
        a = a_ref[b] if 0 <= b < chunk else an_ref[b + GHOST if b < 0 else b - chunk + GHOST]
        coupled = product(a, [(column(n, b) + 2 * GHOST) * size for n in range(slots)], v0_ref, size)
        store_split(v1_ref, at - GHOST * size, divide(s_ref[at : at + size, :] - coupled, at))
    for b in range(chunk):
        at = (b + 2 * GHOST) * size
        coupled = product(a_ref[b], [(column(n, b) + GHOST) * size for n in range(slots)], v1_ref, size)
        store_split(y_ref, b * size, divide(s_ref[at : at + size, :] - coupled, at))
    change = lax.dot_general(back_ref[flip], y_ref[...], (((1,), (1,)), ((), ())), preferred_element_type=F32)
    out_ref[...] = change


def vmem(count):
    return [pl.BlockSpec(memory_space=pltpu.VMEM)] * count


def smem(count):
    return [pl.BlockSpec(memory_space=pltpu.SMEM)] * count


def cost(microseconds):
    return pl.CostEstimate(flops=0, transcendentals=0, bytes_accessed=3_000_000 * microseconds)


PARAMS = pltpu.CompilerParams(vmem_limit_bytes=16 * 1024 * 1024)
BLOCKS_PARAMS = pltpu.CompilerParams(vmem_limit_bytes=48 * 1024 * 1024)


def local(start_state, forcing, iterate, blocks, columns, kdiag):
    steps, rows_dev = iterate.shape
    block_rows, size, width = blocks.shape
    slots = width // size
    n_tm, n_space = lax.axis_size("tm"), lax.axis_size("space")
    total = steps * n_tm
    chunk = block_rows // n_tm
    rows = chunk * size
    edge = GHOST * size
    wide = 2 * edge
    dims = (size, slots, chunk, total, steps)
    order = there_and_back(n_tm)

    tm_index, space_index = lax.axis_index("tm"), lax.axis_index("space")
    flipped = space_index % 2 == 1
    spot = jnp.where(tm_index % 2 == 0, tm_index // 2, n_tm - 1 - tm_index // 2)
    spot = jnp.where(flipped, n_tm - 1 - spot, spot)
    even = (space_index * n_tm + spot) % 2 == 0

    groups, ring = [], []
    for s in range(n_space):
        members = [t * n_space + s for t in (order if s % 2 == 0 else order[::-1])]
        groups.append(tuple(members))
        ring += members
    groups = tuple(groups)
    count = len(ring)

    def deal(value):
        return lax.all_to_all(value, AXES, 0, 0, axis_index_groups=groups, tiled=True)

    def ring_pairs(first):
        pairs = []
        for i in range(first, count - 1, 2):
            pairs += [(ring[i], ring[i + 1]), (ring[i + 1], ring[i])]
        return pairs

    def neighbours(value, hops):
        if hops == 1:
            return [lax.ppermute(value, AXES, ring_pairs(first))[None] for first in (0, 1)]
        left, right = [], []
        for hop in range(1, hops + 1):
            up = [(ring[i], ring[i + hop]) for i in range(count - hop)]
            left.insert(0, lax.ppermute(value, AXES, up))
            right.append(lax.ppermute(value, AXES, [(j, i) for i, j in up]))
        return jnp.stack(left), jnp.stack(right)

    times = [[t * steps + j for t in members for j in range(steps)] for members in (order, order[::-1])]
    made = [tables(total, at) for at in times]
    fwd = np.stack([made[0][0], made[1][0]])
    back = np.stack([made[0][1], made[1][1]])
    lasts = [[at.index(at[j] - 1) // steps if at[j] else -1 for j in range(0, total, steps)] for at in times]
    base = space_index * block_rows + spot * chunk
    hops = wide // rows
    here = [spot, flipped, base, even & (hops == 1), spot, space_index * block_rows, space_index % 2 == 0, tm_index == 0]
    where = jnp.stack([jnp.asarray(value, jnp.int32) for value in here])
    columns = columns.T

    given = pl.pallas_call(
        sides_kernel,
        in_specs=smem(1) + vmem(1) + [pl.BlockSpec(memory_space=pl.ANY)],
        out_specs=vmem(2),
        out_shape=[jax.ShapeDtypeStruct((steps, edge), F32)] * 2,
        compiler_params=BLOCKS_PARAMS,
        name="sides",
    )(where, iterate, blocks)
    sides = []
    for first in (0, 1):
        pairs = [(s, s + 1) for s in range(first, n_space - 1, 2)]
        sides.append(lax.ppermute(given[first], "space", pairs + [(j, i) for i, j in pairs]))
    inner = pl.pallas_call(
        inner_kernel,
        in_specs=smem(2) + vmem(2),
        out_specs=vmem(1)[0],
        out_shape=jax.ShapeDtypeStruct((steps, rows_dev), F32),
        scratch_shapes=[pltpu.VMEM((block_rows, 2 * steps, 2 * size), BF16)] * 2,
        compiler_params=PARAMS,
        name="inner",
    )(where, columns, iterate, blocks)
    tall = rows // 128
    height = -(-(steps + 2) * tall // 8) * 8
    residual, rim = pl.pallas_call(
        outer_kernel,
        in_specs=smem(2) + vmem(8),
        out_specs=vmem(2),
        out_shape=[
            jax.ShapeDtypeStruct((n_tm, height, 128), F32),
            jax.ShapeDtypeStruct((edge + 8, width), F32),
        ],
        scratch_shapes=[pltpu.VMEM((block_rows + 2 * GHOST, 2 * steps, 2 * size), BF16)] * 2
        + [pltpu.VMEM((block_rows // 2, steps, 128), F32)],
        compiler_params=PARAMS,
        cost_estimate=cost(1),
        name="outer",
    )(where, columns, iterate, forcing, blocks, inner, *sides, start_state.reshape(-1, 128), kdiag.reshape(-1, 128))
    residual = deal(residual)

    def rim_columns(value):
        return value[edge, : GHOST * slots].reshape(slots, GHOST).astype(jnp.int32)

    if chunk >= 2 * GHOST and n_tm > 1:
        pairs = []
        for s in range(n_space - 1):
            i, j = ring[(s + 1) * n_tm - 1], ring[(s + 1) * n_tm]
            pairs += [(i, j), (j, i)]
        rim = lax.ppermute(rim, AXES, pairs)
        columns_halo = jnp.concatenate([rim_columns(rim)] * 2, axis=1)
    else:
        up = [(s, s + 1) for s in range(n_space - 1)]
        down = [(j, i) for i, j in up]
        rim = [
            lax.ppermute(value, "space", pairs)
            for value, pairs in ((blocks[-GHOST:], up), (columns[:, -GHOST:], up), (blocks[:GHOST], down), (columns[:, :GHOST], down))
        ]
        columns_halo = jnp.concatenate(rim[1::2], axis=1)
        rim = jnp.concatenate([value.reshape(edge, width) for value in rim[::2]], axis=0)
    a_own, a_near = pl.pallas_call(
        blocks_kernel,
        in_specs=smem(1) + [pl.BlockSpec(memory_space=pl.ANY)] + vmem(1),
        out_specs=vmem(2),
        out_shape=[jax.ShapeDtypeStruct((n, 2 * size, width), BF16) for n in (chunk, 2 * GHOST)],
        scratch_shapes=[
            pltpu.VMEM((chunk + 2 * GHOST, size, width), F32),
            pltpu.SemaphoreType.DMA((chunk + 2 * GHOST,)),
        ],
        compiler_params=BLOCKS_PARAMS,
        cost_estimate=cost(2),
        name="blocks",
    )(where, blocks, rim)

    one, two = neighbours(residual, hops)
    span = rows + 2 * wide
    result = pl.pallas_call(
        functools.partial(sweeps_kernel, dims, lasts),
        in_specs=smem(3) + vmem(8),
        out_specs=vmem(1)[0],
        out_shape=jax.ShapeDtypeStruct((total, rows), F32),
        scratch_shapes=[pltpu.VMEM((span, 2 * total), F32)] * 3
        + [pltpu.VMEM((height, 4 * total), BF16) for height in (span, span - wide, rows)],
        compiler_params=PARAMS,
        cost_estimate=cost(3),
        name="sweeps",
    )(where, columns, columns_halo, a_own, a_near, residual, one, two, fwd, back, made[0][2])

    returned = deal(result.reshape(n_tm, steps, rows))
    return iterate + returned.transpose(1, 0, 2).reshape(steps, rows_dev)


def solution(mesh):
    placed = (
        P("space"),
        P("tm", "space"),
        P("tm", "space"),
        P("space", None, None),
        P("space", None),
        P("space"),
    )
    return jax.shard_map(local, mesh=mesh, in_specs=placed, out_specs=P("tm", "space"), check_vma=False)
```

```python
import functools
import math

import jax
import jax.numpy as jnp
import numpy as np
from jax import lax
from jax.experimental import pallas as pl
from jax.experimental.pallas import tpu as pltpu
from jax.sharding import PartitionSpec as P

GHOST = 4
CORNER_WEIGHT = 0.05
AXES = ("tm", "space")
F32 = jnp.float32
BF16 = jnp.bfloat16


def there_and_back(count):
    return list(range(0, count, 2)) + list(range(count - 1 - count % 2, 0, -2))


def split(value):
    high = value.astype(BF16)
    return high, (value - high.astype(F32)).astype(BF16)


def np_split(value):
    high = value.astype(np.float32).astype(BF16)
    return high, (value - high.astype(np.float64)).astype(np.float32).astype(BF16)


def tables(total, times):
    half = total // 2
    freq = np.arange(half)
    t = np.asarray(times)[:, None]
    angle = 2.0 * math.pi * ((t * freq[None]) % total) / total
    nyquist = np.where(t % 2 == 0, 1.0, -1.0)
    cos, sin = np.cos(angle), np.sin(angle)
    grow = CORNER_WEIGHT ** (t / total)

    def swapped(value):
        return np.roll(value, half, axis=1)

    forward = np.concatenate([cos, nyquist, -sin[:, 1:]], axis=1) * grow
    high, low = np_split(np.concatenate([forward, swapped(forward)], axis=1))
    forward = np.concatenate([high, low], axis=1)
    twice = np.where(freq == 0, 1.0, 2.0)[None]
    high, low = np_split(np.concatenate([twice * cos, nyquist, -2.0 * sin[:, 1:]], axis=1) / grow / total)
    back = np.concatenate([high, swapped(low)] * 2, axis=1)
    root = CORNER_WEIGHT ** (1.0 / total)
    theta = 2.0 * math.pi * freq / total
    lam_re = np.concatenate([1.0 - root * np.cos(theta), [1.0 + root], 1.0 - root * np.cos(theta[1:])])
    lam_im = np.concatenate([root * np.sin(theta), [0.0], -root * np.sin(theta[1:])])
    lam = np.stack([lam_re, lam_im])
    return np.concatenate([forward] * 2, axis=0), back, np.concatenate([lam, swapped(lam)], axis=1).astype(np.float32)


def place(lower_ref, upper_ref, at, value):
    half = value.shape[1] // 2
    turned = pltpu.roll(value, half, 1)
    low = lax.broadcasted_iota(jnp.int32, value.shape, 1) < half
    for i, (first, second) in enumerate(((value, turned), (turned, value))):
        for ref, part in ((lower_ref, jnp.where(low, first, 0.0)), (upper_ref, jnp.where(low, 0.0, second))):
            ref[at + i] = jnp.concatenate(split(part), axis=0)


def couple(block, at, lower_ref, upper_ref):
    size, width = block.shape
    tiles = [lower_ref[at[n]] + upper_ref[at[n + 1]] for n in range(0, len(at) - 1, 2)]
    if len(at) % 2:
        tiles.append(lower_ref[at[-1]])
    picked = jnp.concatenate(tiles, axis=1)[:, :width]
    out = lax.dot_general(
        picked, jnp.concatenate(split(block), axis=0), (((1,), (1,)), ((), ())), preferred_element_type=F32
    )
    steps = out.shape[0] // 2
    out = out[:steps] + out[steps:]
    return out + pltpu.roll(out, size, 1)


def couple_rows(blocks_ref, origin, cols_ref, base, rows, lower_ref, upper_ref, put):
    slots = cols_ref.shape[0]
    size = blocks_ref.shape[1]
    for b in rows:
        pair = [
            couple(blocks_ref[i - origin], [cols_ref[n, i] - base for n in range(slots)], lower_ref, upper_ref)
            for i in (b, b + 1)
        ]
        low = lax.broadcasted_iota(jnp.int32, pair[0].shape, 1) < size
        put(b // 2, jnp.where(low, pair[0], pair[1]))


def sides_kernel(where_ref, x_ref, blocks_ref, one_ref, two_ref):
    even = where_ref[6] == 1
    extent = one_ref.shape[1]
    low, high = x_ref[:, :extent], x_ref[:, x_ref.shape[1] - extent :]
    one_ref[...] = jnp.where(even, high, low)
    two_ref[...] = jnp.where(even, low, high)


def inner_kernel(where_ref, cols_ref, x_ref, blocks_ref, out_ref, lower_ref, upper_ref):
    block_rows = blocks_ref.shape[0]

    def put(i, value):
        out_ref[:, i * 128 : (i + 1) * 128] = value

    for b in range(0, block_rows, 2):
        place(lower_ref, upper_ref, b, x_ref[:, b * 64 : b * 64 + 128])
    rows = range(GHOST, block_rows - GHOST, 2)
    couple_rows(blocks_ref, 0, cols_ref, where_ref[5], rows, lower_ref, upper_ref, put)


def outer_kernel(
    where_ref, cols_ref, x_ref, f_ref, blocks_ref, inner_ref, two_ref, one_ref, start_ref, kd_ref, out_ref, rim_ref,
    lower_ref, upper_ref, edge_ref,
):
    block_rows = cols_ref.shape[1]
    steps = x_ref.shape[0]
    peers, height, _ = out_ref.shape
    tall = x_ref.shape[1] // peers // 128
    even, opening = where_ref[6] == 1, where_ref[7] == 1
    for i in range(0, GHOST, 2):
        lanes = slice(i * 64, i * 64 + 128)
        first, second = one_ref[:, lanes], two_ref[:, lanes]
        place(lower_ref, upper_ref, i, jnp.where(even, second, first))
        place(lower_ref, upper_ref, GHOST + block_rows + i, jnp.where(even, first, second))
    ends = list(range(0, 2 * GHOST, 2)) + list(range(block_rows - 2 * GHOST, block_rows, 2))
    for b in ends:
        place(lower_ref, upper_ref, GHOST + b, x_ref[:, b * 64 : b * 64 + 128])

    def put(i, value):
        edge_ref[i] = value

    outer = [b for b in ends if b < GHOST or b >= block_rows - GHOST]
    couple_rows(blocks_ref, 0, cols_ref, where_ref[5] - GHOST, outer, lower_ref, upper_ref, put)
    for i in range(x_ref.shape[1] // 128):
        lanes = slice(i * 128, (i + 1) * 128)
        now = x_ref[:, lanes]
        coupled = edge_ref[i] if 2 * i in outer else inner_ref[:, lanes]
        kd = kd_ref[i : i + 1, :]
        before = jnp.where(opening, start_ref[i : i + 1, :], 0.0)
        previous = jnp.concatenate([before, now[: steps - 1]], axis=0)
        p, j = i // tall, i % tall
        out_ref[p, j * steps : (j + 1) * steps, :] = f_ref[:, lanes] + previous - (1.0 + kd) * now - coupled
        out_ref[p, steps * tall + j : steps * tall + j + 1, :] = now[steps - 1 :]
        out_ref[p, (steps + 1) * tall + j : (steps + 1) * tall + j + 1, :] = kd
    used = (steps + 2) * tall
    if used < height:
        out_ref[:, used:, :] = jnp.zeros((peers, height - used, 128), F32)

    lowest = where_ref[0] == 0
    _, size, width = blocks_ref.shape
    slots = width // size
    lane = lax.broadcasted_iota(jnp.int32, (8, width), 1)
    found = jnp.zeros((8, width), jnp.int32)
    for b in range(GHOST):
        last = block_rows - GHOST + b
        rim_ref[b * size : (b + 1) * size, :] = jnp.where(lowest, blocks_ref[b], blocks_ref[last])
        for n in range(slots):
            found = jnp.where(lane == n * GHOST + b, cols_ref[n, jnp.where(lowest, b, last)], found)
    rim_ref[GHOST * size :, :] = found.astype(F32)


def blocks_kernel(where_ref, blocks_ref, rim_ref, own_ref, near_ref, buffer, sems):
    count, size, _ = buffer.shape
    chunk = count - 2 * GHOST
    block_rows = blocks_ref.shape[0]
    spot = where_ref[0]
    rows = list(range(GHOST, GHOST + chunk)) + list(range(GHOST)) + list(range(GHOST + chunk, count))
    copies = {}
    for b in rows:
        row = jnp.clip(spot * chunk + b - GHOST, 0, block_rows - 1)
        copies[b] = pltpu.make_async_copy(blocks_ref.at[row], buffer.at[b], sems.at[b])
        copies[b].start()
    for b in rows:
        copies[b].wait()
        value = buffer[b]
        if GHOST <= b < GHOST + chunk:
            ref, at = own_ref, b - GHOST
        else:
            ref, at = near_ref, b if b < GHOST else b - chunk
            row = spot * chunk + b - GHOST
            if rim_ref.shape[0] > GHOST * size + 8:
                at_rim = jnp.where(row < 0, row + GHOST, GHOST + row - block_rows)
            else:
                at_rim = jnp.where(row < 0, row + GHOST, row - block_rows)
            outside = (row < 0) | (row >= block_rows)
            at_rim = pl.multiple_of(jnp.where(outside, at_rim, 0) * size, size)
            value = jnp.where(outside, rim_ref[pl.ds(at_rim, size), :], value)
        high, low = split(value)
        ref[at, :size] = high
        ref[at, size:] = low


def product(a, at, v_ref, size):
    picked = jnp.concatenate([v_ref[pl.ds(pl.multiple_of(row, size), size), :] for row in at], axis=0)
    out = jnp.dot(a, picked, preferred_element_type=F32)
    out = out[:size] + out[size:]
    half = out.shape[1] // 2
    return out[:, :half] + out[:, half:]


def store_split(ref, at, value):
    high, low = split(value)
    rows, channels = value.shape
    half = ref.shape[1] // 2
    ref[at : at + rows, :channels] = high
    ref[at : at + rows, half : half + channels] = low


def gather_chunk(pick, crossed, flip, lasts, dims):
    size, slots, chunk, total, steps = dims
    tall = chunk * size // 128
    count = total // steps
    parts = []
    for j in range(count):
        last = jnp.where(flip == 1, lasts[1][j], lasts[0][j])
        at = jnp.maximum(last, 0)
        held = pick(jnp.where(crossed, count - 1 - j, j))
        other = pick(jnp.where(crossed, count - 1 - at, at))
        wide = [held[i * steps : (i + 1) * steps] for i in range(tall)]
        before = [other[steps * tall + i : steps * tall + i + 1] for i in range(tall)]
        wide, before = jnp.concatenate(wide, axis=1), jnp.concatenate(before, axis=1)
        opens = lax.broadcasted_iota(jnp.int32, wide.shape, 0) == 0
        parts.append(wide + jnp.where(opens & (last >= 0), before, 0.0))
    kd = jnp.concatenate([held[(steps + 1) * tall + i : (steps + 1) * tall + i + 1] for i in range(tall)], axis=1)
    return jnp.concatenate(parts, axis=0), kd


def sweeps_kernel(
    dims, lasts, where_ref, cols_ref, near_ref, a_ref, an_ref, r_ref, one_ref, two_ref, fwd_ref, back_ref, lam_ref, out_ref,
    s_ref, cr_ref, ci_ref, v0_ref, v1_ref, y_ref,
):
    size, slots, chunk, total, steps = dims
    rows = chunk * size
    wide = 2 * GHOST * size
    spot, flip, base, even = where_ref[0], where_ref[1], where_ref[2], where_ref[3] == 1
    count = total // steps
    block_rows = cols_ref.shape[1]
    fwd = fwd_ref[flip]

    def forward(at, value):
        high, low = split(value)
        stacked = jnp.concatenate([high, low], axis=0)
        out = lax.dot_general(stacked, fwd, (((0,), (0,)), ((), ())), preferred_element_type=F32)
        s_ref[at : at + value.shape[1], :] = out[:, : 2 * total] + out[:, 2 * total :]

    def near(first_ref, second_ref, hop):
        return lambda at: jnp.where(even, second_ref[hop, at], first_ref[hop, at])

    hops = one_ref.shape[0]
    chunks = [(near(one_ref, two_ref, h), spot < hops - h) for h in range(hops)]
    chunks += [(lambda at: r_ref[at], False)]
    chunks += [(near(two_ref, one_ref, h), spot >= count - 1 - h) for h in range(hops)]
    kds = []
    for i, (pick, crossed) in enumerate(chunks):
        residual, kd = gather_chunk(pick, crossed, flip, lasts, dims)
        forward(i * rows, residual)
        kds.append(kd)
    kd = jnp.concatenate(kds, axis=1)
    kd = jnp.broadcast_to(kd, (2 * total, kd.shape[1])).T
    diag = kd + lam_ref[0:1, :]
    imag = lam_ref[1:2, :]
    inverse = 1.0 / (diag * diag + imag * imag)
    cr_ref[...] = diag * inverse
    ci_ref[...] = imag * inverse

    def divide(value, at):
        span = slice(at, at + value.shape[0])
        return value * cr_ref[span, :] + pltpu.roll(value, total, 1) * ci_ref[span, :]

    def column(n, b):
        row = spot * chunk + b
        found = cols_ref[n, jnp.clip(row, 0, block_rows - 1)]
        if b < 0:
            found = jnp.where(row < 0, near_ref[n, jnp.maximum(row + GHOST, 0)], found)
        if b >= chunk:
            found = jnp.where(row >= block_rows, near_ref[n, GHOST + jnp.maximum(row - block_rows, 0)], found)
        return jnp.clip(found - base, -2 * GHOST, chunk + 2 * GHOST - 1)

    store_split(v0_ref, 0, divide(s_ref[...], 0))
    for b in range(-GHOST, chunk + GHOST):
        at = (b + 2 * GHOST) * size
        a = a_ref[b] if 0 <= b < chunk else an_ref[b + GHOST if b < 0 else b - chunk + GHOST]
        coupled = product(a, [(column(n, b) + 2 * GHOST) * size for n in range(slots)], v0_ref, size)
        store_split(v1_ref, at - GHOST * size, divide(s_ref[at : at + size, :] - coupled, at))
    for b in range(chunk):
        at = (b + 2 * GHOST) * size
        coupled = product(a_ref[b], [(column(n, b) + GHOST) * size for n in range(slots)], v1_ref, size)
        store_split(y_ref, b * size, divide(s_ref[at : at + size, :] - coupled, at))
    change = lax.dot_general(back_ref[flip], y_ref[...], (((1,), (1,)), ((), ())), preferred_element_type=F32)
    out_ref[...] = change


def vmem(count):
    return [pl.BlockSpec(memory_space=pltpu.VMEM)] * count


def smem(count):
    return [pl.BlockSpec(memory_space=pltpu.SMEM)] * count


def cost(microseconds):
    return pl.CostEstimate(flops=0, transcendentals=0, bytes_accessed=3_000_000 * microseconds)


PARAMS = pltpu.CompilerParams(vmem_limit_bytes=16 * 1024 * 1024)
BLOCKS_PARAMS = pltpu.CompilerParams(vmem_limit_bytes=48 * 1024 * 1024)


def local(start_state, forcing, iterate, blocks, columns, kdiag):
    steps, rows_dev = iterate.shape
    block_rows, size, width = blocks.shape
    slots = width // size
    n_tm, n_space = lax.axis_size("tm"), lax.axis_size("space")
    total = steps * n_tm
    chunk = block_rows // n_tm
    rows = chunk * size
    edge = GHOST * size
    wide = 2 * edge
    dims = (size, slots, chunk, total, steps)
    order = there_and_back(n_tm)

    tm_index, space_index = lax.axis_index("tm"), lax.axis_index("space")
    flipped = space_index % 2 == 1
    spot = jnp.where(tm_index % 2 == 0, tm_index // 2, n_tm - 1 - tm_index // 2)
    spot = jnp.where(flipped, n_tm - 1 - spot, spot)
    even = (space_index * n_tm + spot) % 2 == 0

    groups, ring = [], []
    for s in range(n_space):
        members = [t * n_space + s for t in (order if s % 2 == 0 else order[::-1])]
        groups.append(tuple(members))
        ring += members
    groups = tuple(groups)
    count = len(ring)

    def deal(value):
        return lax.all_to_all(value, AXES, 0, 0, axis_index_groups=groups, tiled=True)

    def ring_pairs(first):
        pairs = []
        for i in range(first, count - 1, 2):
            pairs += [(ring[i], ring[i + 1]), (ring[i + 1], ring[i])]
        return pairs

    def neighbours(value, hops):
        if hops == 1:
            return [lax.ppermute(value, AXES, ring_pairs(first))[None] for first in (0, 1)]
        left, right = [], []
        for hop in range(1, hops + 1):
            up = [(ring[i], ring[i + hop]) for i in range(count - hop)]
            left.insert(0, lax.ppermute(value, AXES, up))
            right.append(lax.ppermute(value, AXES, [(j, i) for i, j in up]))
        return jnp.stack(left), jnp.stack(right)

    times = [[t * steps + j for t in members for j in range(steps)] for members in (order, order[::-1])]
    made = [tables(total, at) for at in times]
    fwd = np.stack([made[0][0], made[1][0]])
    back = np.stack([made[0][1], made[1][1]])
    lasts = [[at.index(at[j] - 1) // steps if at[j] else -1 for j in range(0, total, steps)] for at in times]
    base = space_index * block_rows + spot * chunk
    hops = wide // rows
    here = [spot, flipped, base, even & (hops == 1), spot, space_index * block_rows, space_index % 2 == 0, tm_index == 0]
    where = jnp.stack([jnp.asarray(value, jnp.int32) for value in here])
    columns = columns.T

    given = pl.pallas_call(
        sides_kernel,
        in_specs=smem(1) + vmem(1) + [pl.BlockSpec(memory_space=pl.ANY)],
        out_specs=vmem(2),
        out_shape=[jax.ShapeDtypeStruct((steps, edge), F32)] * 2,
        compiler_params=BLOCKS_PARAMS,
        name="sides",
    )(where, iterate, blocks)
    sides = []
    for first in (1, 0):
        pairs = [(s, s + 1) for s in range(first, n_space - 1, 2)]
        sides.insert(0, lax.ppermute(given[first], "space", pairs + [(j, i) for i, j in pairs]))
    inner = pl.pallas_call(
        inner_kernel,
        in_specs=smem(2) + vmem(2),
        out_specs=vmem(1)[0],
        out_shape=jax.ShapeDtypeStruct((steps, rows_dev), F32),
        scratch_shapes=[pltpu.VMEM((block_rows, 2 * steps, 2 * size), BF16)] * 2,
        compiler_params=PARAMS,
        name="inner",
    )(where, columns, iterate, blocks)
    tall = rows // 128
    height = -(-(steps + 2) * tall // 8) * 8
    residual, rim = pl.pallas_call(
        outer_kernel,
        in_specs=smem(2) + vmem(8),
        out_specs=vmem(2),
        out_shape=[
            jax.ShapeDtypeStruct((n_tm, height, 128), F32),
            jax.ShapeDtypeStruct((edge + 8, width), F32),
        ],
        scratch_shapes=[pltpu.VMEM((block_rows + 2 * GHOST, 2 * steps, 2 * size), BF16)] * 2
        + [pltpu.VMEM((block_rows // 2, steps, 128), F32)],
        compiler_params=PARAMS,
        cost_estimate=cost(1),
        name="outer",
    )(where, columns, iterate, forcing, blocks, inner, *sides[::-1], start_state.reshape(-1, 128), kdiag.reshape(-1, 128))
    residual = deal(residual)

    def rim_columns(value):
        return value[edge, : GHOST * slots].reshape(slots, GHOST).astype(jnp.int32)

    if chunk >= 2 * GHOST and n_tm > 1:
        pairs = []
        for s in range(n_space - 1):
            i, j = ring[(s + 1) * n_tm - 1], ring[(s + 1) * n_tm]
            pairs += [(i, j), (j, i)]
        rim = lax.ppermute(rim, AXES, pairs)
        columns_halo = jnp.concatenate([rim_columns(rim)] * 2, axis=1)
    else:
        up = [(s, s + 1) for s in range(n_space - 1)]
        down = [(j, i) for i, j in up]
        rim = [
            lax.ppermute(value, "space", pairs)
            for value, pairs in ((blocks[-GHOST:], up), (columns[:, -GHOST:], up), (blocks[:GHOST], down), (columns[:, :GHOST], down))
        ]
        columns_halo = jnp.concatenate(rim[1::2], axis=1)
        rim = jnp.concatenate([value.reshape(edge, width) for value in rim[::2]], axis=0)
    a_own, a_near = pl.pallas_call(
        blocks_kernel,
        in_specs=smem(1) + [pl.BlockSpec(memory_space=pl.ANY)] + vmem(1),
        out_specs=vmem(2),
        out_shape=[jax.ShapeDtypeStruct((n, 2 * size, width), BF16) for n in (chunk, 2 * GHOST)],
        scratch_shapes=[
            pltpu.VMEM((chunk + 2 * GHOST, size, width), F32),
            pltpu.SemaphoreType.DMA((chunk + 2 * GHOST,)),
        ],
        compiler_params=BLOCKS_PARAMS,
        cost_estimate=cost(2),
        name="blocks",
    )(where, blocks, rim)

    one, two = neighbours(residual, hops)
    span = rows + 2 * wide
    result = pl.pallas_call(
        functools.partial(sweeps_kernel, dims, lasts),
        in_specs=smem(3) + vmem(8),
        out_specs=vmem(1)[0],
        out_shape=jax.ShapeDtypeStruct((total, rows), F32),
        scratch_shapes=[pltpu.VMEM((span, 2 * total), F32)] * 3
        + [pltpu.VMEM((height, 4 * total), BF16) for height in (span, span - wide, rows)],
        compiler_params=PARAMS,
        cost_estimate=cost(3),
        name="sweeps",
    )(where, columns, columns_halo, a_own, a_near, residual, one, two, fwd, back, made[0][2])

    returned = deal(result.reshape(n_tm, steps, rows))
    return iterate + returned.transpose(1, 0, 2).reshape(steps, rows_dev)


def solution(mesh):
    placed = (
        P("space"),
        P("tm", "space"),
        P("tm", "space"),
        P("space", None, None),
        P("space", None),
        P("space"),
    )
    return jax.shard_map(local, mesh=mesh, in_specs=placed, out_specs=P("tm", "space"), check_vma=False)
```

```python
import functools
import math

import jax
import jax.numpy as jnp
import numpy as np
from jax import lax
from jax.experimental import pallas as pl
from jax.experimental.pallas import tpu as pltpu
from jax.sharding import PartitionSpec as P

GHOST = 4
CORNER_WEIGHT = 0.05
AXES = ("tm", "space")
F32 = jnp.float32
BF16 = jnp.bfloat16


def there_and_back(count):
    return list(range(0, count, 2)) + list(range(count - 1 - count % 2, 0, -2))


def split(value):
    high = value.astype(BF16)
    return high, (value - high.astype(F32)).astype(BF16)


def np_split(value):
    high = value.astype(np.float32).astype(BF16)
    return high, (value - high.astype(np.float64)).astype(np.float32).astype(BF16)


def tables(total, times):
    half = total // 2
    freq = np.arange(half)
    t = np.asarray(times)[:, None]
    angle = 2.0 * math.pi * ((t * freq[None]) % total) / total
    nyquist = np.where(t % 2 == 0, 1.0, -1.0)
    cos, sin = np.cos(angle), np.sin(angle)
    grow = CORNER_WEIGHT ** (t / total)

    def swapped(value):
        return np.roll(value, half, axis=1)

    forward = np.concatenate([cos, nyquist, -sin[:, 1:]], axis=1) * grow
    high, low = np_split(np.concatenate([forward, swapped(forward)], axis=1))
    forward = np.concatenate([high, low], axis=1)
    twice = np.where(freq == 0, 1.0, 2.0)[None]
    high, low = np_split(np.concatenate([twice * cos, nyquist, -2.0 * sin[:, 1:]], axis=1) / grow / total)
    back = np.concatenate([high, swapped(low)] * 2, axis=1)
    root = CORNER_WEIGHT ** (1.0 / total)
    theta = 2.0 * math.pi * freq / total
    lam_re = np.concatenate([1.0 - root * np.cos(theta), [1.0 + root], 1.0 - root * np.cos(theta[1:])])
    lam_im = np.concatenate([root * np.sin(theta), [0.0], -root * np.sin(theta[1:])])
    lam = np.stack([lam_re, lam_im])
    return np.concatenate([forward] * 2, axis=0), back, np.concatenate([lam, swapped(lam)], axis=1).astype(np.float32)


def place(lower_ref, upper_ref, at, value):
    half = value.shape[1] // 2
    turned = pltpu.roll(value, half, 1)
    low = lax.broadcasted_iota(jnp.int32, value.shape, 1) < half
    for i, (first, second) in enumerate(((value, turned), (turned, value))):
        for ref, part in ((lower_ref, jnp.where(low, first, 0.0)), (upper_ref, jnp.where(low, 0.0, second))):
            ref[at + i] = jnp.concatenate(split(part), axis=0)


def couple(block, at, lower_ref, upper_ref):
    size, width = block.shape
    tiles = [lower_ref[at[n]] + upper_ref[at[n + 1]] for n in range(0, len(at) - 1, 2)]
    if len(at) % 2:
        tiles.append(lower_ref[at[-1]])
    picked = jnp.concatenate(tiles, axis=1)[:, :width]
    out = lax.dot_general(
        picked, jnp.concatenate(split(block), axis=0), (((1,), (1,)), ((), ())), preferred_element_type=F32
    )
    steps = out.shape[0] // 2
    out = out[:steps] + out[steps:]
    return out + pltpu.roll(out, size, 1)


def couple_rows(blocks_ref, origin, cols_ref, base, rows, lower_ref, upper_ref, put):
    slots = cols_ref.shape[0]
    size = blocks_ref.shape[1]
    for b in rows:
        pair = [
            couple(blocks_ref[i - origin], [cols_ref[n, i] - base for n in range(slots)], lower_ref, upper_ref)
            for i in (b, b + 1)
        ]
        low = lax.broadcasted_iota(jnp.int32, pair[0].shape, 1) < size
        put(b // 2, jnp.where(low, pair[0], pair[1]))


def sides_kernel(where_ref, x_ref, blocks_ref, one_ref, two_ref):
    even = where_ref[6] == 1
    extent = one_ref.shape[1]
    low, high = x_ref[:, :extent], x_ref[:, x_ref.shape[1] - extent :]
    one_ref[...] = jnp.where(even, high, low)
    two_ref[...] = jnp.where(even, low, high)


def inner_kernel(where_ref, cols_ref, x_ref, blocks_ref, out_ref, lower_ref, upper_ref):
    block_rows = blocks_ref.shape[0]

    def put(i, value):
        out_ref[:, i * 128 : (i + 1) * 128] = value

    for b in range(0, block_rows, 2):
        place(lower_ref, upper_ref, b, x_ref[:, b * 64 : b * 64 + 128])
    rows = range(GHOST, block_rows - GHOST, 2)
    couple_rows(blocks_ref, 0, cols_ref, where_ref[5], rows, lower_ref, upper_ref, put)


def outer_kernel(
    where_ref, cols_ref, x_ref, f_ref, blocks_ref, inner_ref, two_ref, one_ref, start_ref, kd_ref, out_ref, rim_ref,
    lower_ref, upper_ref, edge_ref,
):
    block_rows = cols_ref.shape[1]
    steps = x_ref.shape[0]
    peers, height, _ = out_ref.shape
    tall = x_ref.shape[1] // peers // 128
    even, opening = where_ref[6] == 1, where_ref[7] == 1
    for i in range(0, GHOST, 2):
        lanes = slice(i * 64, i * 64 + 128)
        first, second = one_ref[:, lanes], two_ref[:, lanes]
        place(lower_ref, upper_ref, i, jnp.where(even, second, first))
        place(lower_ref, upper_ref, GHOST + block_rows + i, jnp.where(even, first, second))
    ends = list(range(0, 2 * GHOST, 2)) + list(range(block_rows - 2 * GHOST, block_rows, 2))
    for b in ends:
        place(lower_ref, upper_ref, GHOST + b, x_ref[:, b * 64 : b * 64 + 128])

    def put(i, value):
        edge_ref[i] = value

    outer = [b for b in ends if b < GHOST or b >= block_rows - GHOST]
    couple_rows(blocks_ref, 0, cols_ref, where_ref[5] - GHOST, outer, lower_ref, upper_ref, put)
    for i in range(x_ref.shape[1] // 128):
        lanes = slice(i * 128, (i + 1) * 128)
        now = x_ref[:, lanes]
        coupled = edge_ref[i] if 2 * i in outer else inner_ref[:, lanes]
        kd = kd_ref[i : i + 1, :]
        before = jnp.where(opening, start_ref[i : i + 1, :], 0.0)
        previous = jnp.concatenate([before, now[: steps - 1]], axis=0)
        p, j = i // tall, i % tall
        out_ref[p, j * steps : (j + 1) * steps, :] = f_ref[:, lanes] + previous - (1.0 + kd) * now - coupled
        out_ref[p, steps * tall + j : steps * tall + j + 1, :] = now[steps - 1 :]
        out_ref[p, (steps + 1) * tall + j : (steps + 1) * tall + j + 1, :] = kd
    used = (steps + 2) * tall
    if used < height:
        out_ref[:, used:, :] = jnp.zeros((peers, height - used, 128), F32)

    lowest = where_ref[0] == 0
    _, size, width = blocks_ref.shape
    slots = width // size
    lane = lax.broadcasted_iota(jnp.int32, (8, width), 1)
    found = jnp.zeros((8, width), jnp.int32)
    for b in range(GHOST):
        last = block_rows - GHOST + b
        rim_ref[b * size : (b + 1) * size, :] = jnp.where(lowest, blocks_ref[b], blocks_ref[last])
        for n in range(slots):
            found = jnp.where(lane == n * GHOST + b, cols_ref[n, jnp.where(lowest, b, last)], found)
    rim_ref[GHOST * size :, :] = found.astype(F32)


def blocks_kernel(where_ref, blocks_ref, rim_ref, own_ref, near_ref, buffer, sems):
    count, size, _ = buffer.shape
    chunk = count - 2 * GHOST
    block_rows = blocks_ref.shape[0]
    spot = where_ref[0]
    rows = list(range(GHOST, GHOST + chunk)) + list(range(GHOST)) + list(range(GHOST + chunk, count))
    copies = {}
    for b in rows:
        row = jnp.clip(spot * chunk + b - GHOST, 0, block_rows - 1)
        copies[b] = pltpu.make_async_copy(blocks_ref.at[row], buffer.at[b], sems.at[b])
        copies[b].start()
    for b in rows:
        copies[b].wait()
        value = buffer[b]
        if GHOST <= b < GHOST + chunk:
            ref, at = own_ref, b - GHOST
        else:
            ref, at = near_ref, b if b < GHOST else b - chunk
            row = spot * chunk + b - GHOST
            if rim_ref.shape[0] > GHOST * size + 8:
                at_rim = jnp.where(row < 0, row + GHOST, GHOST + row - block_rows)
            else:
                at_rim = jnp.where(row < 0, row + GHOST, row - block_rows)
            outside = (row < 0) | (row >= block_rows)
            at_rim = pl.multiple_of(jnp.where(outside, at_rim, 0) * size, size)
            value = jnp.where(outside, rim_ref[pl.ds(at_rim, size), :], value)
        high, low = split(value)
        ref[at, :size] = high
        ref[at, size:] = low


def product(a, at, v_ref, size):
    picked = jnp.concatenate([v_ref[pl.ds(pl.multiple_of(row, size), size), :] for row in at], axis=0)
    out = jnp.dot(a, picked, preferred_element_type=F32)
    out = out[:size] + out[size:]
    half = out.shape[1] // 2
    return out[:, :half] + out[:, half:]


def store_split(ref, at, value):
    high, low = split(value)
    rows, channels = value.shape
    half = ref.shape[1] // 2
    ref[at : at + rows, :channels] = high
    ref[at : at + rows, half : half + channels] = low


def gather_chunk(pick, crossed, flip, lasts, dims):
    size, slots, chunk, total, steps = dims
    tall = chunk * size // 128
    count = total // steps
    parts = []
    for j in range(count):
        last = jnp.where(flip == 1, lasts[1][j], lasts[0][j])
        at = jnp.maximum(last, 0)
        held = pick(jnp.where(crossed, count - 1 - j, j))
        other = pick(jnp.where(crossed, count - 1 - at, at))
        wide = [held[i * steps : (i + 1) * steps] for i in range(tall)]
        before = [other[steps * tall + i : steps * tall + i + 1] for i in range(tall)]
        wide, before = jnp.concatenate(wide, axis=1), jnp.concatenate(before, axis=1)
        opens = lax.broadcasted_iota(jnp.int32, wide.shape, 0) == 0
        parts.append(wide + jnp.where(opens & (last >= 0), before, 0.0))
    kd = jnp.concatenate([held[(steps + 1) * tall + i : (steps + 1) * tall + i + 1] for i in range(tall)], axis=1)
    return jnp.concatenate(parts, axis=0), kd


def sweeps_kernel(
    dims, lasts, where_ref, cols_ref, near_ref, a_ref, an_ref, r_ref, one_ref, two_ref, fwd_ref, back_ref, lam_ref, out_ref,
    s_ref, cr_ref, ci_ref, v0_ref, v1_ref, y_ref,
):
    size, slots, chunk, total, steps = dims
    rows = chunk * size
    wide = 2 * GHOST * size
    spot, flip, base, even = where_ref[0], where_ref[1], where_ref[2], where_ref[3] == 1
    count = total // steps
    block_rows = cols_ref.shape[1]
    fwd = fwd_ref[flip]

    def forward(at, value):
        high, low = split(value)
        stacked = jnp.concatenate([high, low], axis=0)
        out = lax.dot_general(stacked, fwd, (((0,), (0,)), ((), ())), preferred_element_type=F32)
        s_ref[at : at + value.shape[1], :] = out[:, : 2 * total] + out[:, 2 * total :]

    def near(first_ref, second_ref, hop):
        return lambda at: jnp.where(even, second_ref[hop, at], first_ref[hop, at])

    hops = one_ref.shape[0]
    chunks = [(near(one_ref, two_ref, h), spot < hops - h) for h in range(hops)]
    chunks += [(lambda at: r_ref[at], False)]
    chunks += [(near(two_ref, one_ref, h), spot >= count - 1 - h) for h in range(hops)]
    kds = []
    for i, (pick, crossed) in enumerate(chunks):
        residual, kd = gather_chunk(pick, crossed, flip, lasts, dims)
        forward(i * rows, residual)
        kds.append(kd)
    kd = jnp.concatenate(kds, axis=1)
    kd = jnp.broadcast_to(kd, (2 * total, kd.shape[1])).T
    diag = kd + lam_ref[0:1, :]
    imag = lam_ref[1:2, :]
    inverse = 1.0 / (diag * diag + imag * imag)
    cr_ref[...] = diag * inverse
    ci_ref[...] = imag * inverse

    def divide(value, at):
        span = slice(at, at + value.shape[0])
        return value * cr_ref[span, :] + pltpu.roll(value, total, 1) * ci_ref[span, :]

    def column(n, b):
        row = spot * chunk + b
        found = cols_ref[n, jnp.clip(row, 0, block_rows - 1)]
        if b < 0:
            found = jnp.where(row < 0, near_ref[n, jnp.clip(row + GHOST, 0, GHOST - 1)], found)
        if b >= chunk:
            found = jnp.where(row >= block_rows, near_ref[n, GHOST + jnp.clip(row - block_rows, 0, GHOST - 1)], found)
        return jnp.clip(found - base, -2 * GHOST, chunk + 2 * GHOST - 1)

    store_split(v0_ref, 0, divide(s_ref[...], 0))
    for b in range(-GHOST, chunk + GHOST):
        at = (b + 2 * GHOST) * size
        a = a_ref[b] if 0 <= b < chunk else an_ref[b + GHOST if b < 0 else b - chunk + GHOST]
        coupled = product(a, [(column(n, b) + 2 * GHOST) * size for n in range(slots)], v0_ref, size)
        store_split(v1_ref, at - GHOST * size, divide(s_ref[at : at + size, :] - coupled, at))
    for b in range(chunk):
        at = (b + 2 * GHOST) * size
        coupled = product(a_ref[b], [(column(n, b) + GHOST) * size for n in range(slots)], v1_ref, size)
        store_split(y_ref, b * size, divide(s_ref[at : at + size, :] - coupled, at))
    change = lax.dot_general(back_ref[flip], y_ref[...], (((1,), (1,)), ((), ())), preferred_element_type=F32)
    out_ref[...] = change


def vmem(count):
    return [pl.BlockSpec(memory_space=pltpu.VMEM)] * count


def smem(count):
    return [pl.BlockSpec(memory_space=pltpu.SMEM)] * count


def cost(microseconds):
    return pl.CostEstimate(flops=0, transcendentals=0, bytes_accessed=3_000_000 * microseconds)


PARAMS = pltpu.CompilerParams(vmem_limit_bytes=16 * 1024 * 1024)
BLOCKS_PARAMS = pltpu.CompilerParams(vmem_limit_bytes=48 * 1024 * 1024)


def local(start_state, forcing, iterate, blocks, columns, kdiag):
    steps, rows_dev = iterate.shape
    block_rows, size, width = blocks.shape
    slots = width // size
    n_tm, n_space = lax.axis_size("tm"), lax.axis_size("space")
    total = steps * n_tm
    chunk = block_rows // n_tm
    rows = chunk * size
    edge = GHOST * size
    wide = 2 * edge
    dims = (size, slots, chunk, total, steps)
    order = there_and_back(n_tm)

    tm_index, space_index = lax.axis_index("tm"), lax.axis_index("space")
    flipped = space_index % 2 == 1
    spot = jnp.where(tm_index % 2 == 0, tm_index // 2, n_tm - 1 - tm_index // 2)
    spot = jnp.where(flipped, n_tm - 1 - spot, spot)
    even = (space_index * n_tm + spot) % 2 == 0

    groups, ring = [], []
    for s in range(n_space):
        members = [t * n_space + s for t in (order if s % 2 == 0 else order[::-1])]
        groups.append(tuple(members))
        ring += members
    groups = tuple(groups)
    count = len(ring)

    def deal(value):
        return lax.all_to_all(value, AXES, 0, 0, axis_index_groups=groups, tiled=True)

    def ring_pairs(first):
        pairs = []
        for i in range(first, count - 1, 2):
            pairs += [(ring[i], ring[i + 1]), (ring[i + 1], ring[i])]
        return pairs

    def neighbours(value, hops):
        if hops == 1:
            return [lax.ppermute(value, AXES, ring_pairs(first))[None] for first in (0, 1)]
        left, right = [], []
        for hop in range(1, hops + 1):
            up = [(ring[i], ring[i + hop]) for i in range(count - hop)]
            left.insert(0, lax.ppermute(value, AXES, up))
            right.append(lax.ppermute(value, AXES, [(j, i) for i, j in up]))
        return jnp.stack(left), jnp.stack(right)

    times = [[t * steps + j for t in members for j in range(steps)] for members in (order, order[::-1])]
    made = [tables(total, at) for at in times]
    fwd = np.stack([made[0][0], made[1][0]])
    back = np.stack([made[0][1], made[1][1]])
    lasts = [[at.index(at[j] - 1) // steps if at[j] else -1 for j in range(0, total, steps)] for at in times]
    base = space_index * block_rows + spot * chunk
    hops = wide // rows
    here = [spot, flipped, base, even & (hops == 1), spot, space_index * block_rows, space_index % 2 == 0, tm_index == 0]
    where = jnp.stack([jnp.asarray(value, jnp.int32) for value in here])
    columns = columns.T

    given = pl.pallas_call(
        sides_kernel,
        in_specs=smem(1) + vmem(1) + [pl.BlockSpec(memory_space=pl.ANY)],
        out_specs=vmem(2),
        out_shape=[jax.ShapeDtypeStruct((steps, edge), F32)] * 2,
        compiler_params=BLOCKS_PARAMS,
        name="sides",
    )(where, iterate, blocks)
    sides = []
    for first in (1, 0):
        pairs = [(s, s + 1) for s in range(first, n_space - 1, 2)]
        sides.insert(0, lax.ppermute(given[first], "space", pairs + [(j, i) for i, j in pairs]))
    inner = pl.pallas_call(
        inner_kernel,
        in_specs=smem(2) + vmem(2),
        out_specs=vmem(1)[0],
        out_shape=jax.ShapeDtypeStruct((steps, rows_dev), F32),
        scratch_shapes=[pltpu.VMEM((block_rows, 2 * steps, 2 * size), BF16)] * 2,
        compiler_params=PARAMS,
        name="inner",
    )(where, columns, iterate, blocks)
    tall = rows // 128
    height = -(-(steps + 2) * tall // 8) * 8
    residual, rim = pl.pallas_call(
        outer_kernel,
        in_specs=smem(2) + vmem(8),
        out_specs=vmem(2),
        out_shape=[
            jax.ShapeDtypeStruct((n_tm, height, 128), F32),
            jax.ShapeDtypeStruct((edge + 8, width), F32),
        ],
        scratch_shapes=[pltpu.VMEM((block_rows + 2 * GHOST, 2 * steps, 2 * size), BF16)] * 2
        + [pltpu.VMEM((block_rows // 2, steps, 128), F32)],
        compiler_params=PARAMS,
        cost_estimate=cost(1),
        name="outer",
    )(where, columns, iterate, forcing, blocks, inner, *sides[::-1], start_state.reshape(-1, 128), kdiag.reshape(-1, 128))
    residual = deal(residual)

    def rim_columns(value):
        return value[edge, : GHOST * slots].reshape(slots, GHOST).astype(jnp.int32)

    if chunk >= 2 * GHOST and n_tm > 1:
        pairs = []
        for s in range(n_space - 1):
            i, j = ring[(s + 1) * n_tm - 1], ring[(s + 1) * n_tm]
            pairs += [(i, j), (j, i)]
        rim = lax.ppermute(rim, AXES, pairs)
        columns_halo = jnp.concatenate([rim_columns(rim)] * 2, axis=1)
    else:
        up = [(s, s + 1) for s in range(n_space - 1)]
        down = [(j, i) for i, j in up]
        rim = [
            lax.ppermute(value, "space", pairs)
            for value, pairs in ((blocks[-GHOST:], up), (columns[:, -GHOST:], up), (blocks[:GHOST], down), (columns[:, :GHOST], down))
        ]
        columns_halo = jnp.concatenate(rim[1::2], axis=1)
        rim = jnp.concatenate([value.reshape(edge, width) for value in rim[::2]], axis=0)
    a_own, a_near = pl.pallas_call(
        blocks_kernel,
        in_specs=smem(1) + [pl.BlockSpec(memory_space=pl.ANY)] + vmem(1),
        out_specs=vmem(2),
        out_shape=[jax.ShapeDtypeStruct((n, 2 * size, width), BF16) for n in (chunk, 2 * GHOST)],
        scratch_shapes=[
            pltpu.VMEM((chunk + 2 * GHOST, size, width), F32),
            pltpu.SemaphoreType.DMA((chunk + 2 * GHOST,)),
        ],
        compiler_params=BLOCKS_PARAMS,
        cost_estimate=cost(2),
        name="blocks",
    )(where, blocks, rim)

    one, two = neighbours(residual, hops)
    span = rows + 2 * wide
    result = pl.pallas_call(
        functools.partial(sweeps_kernel, dims, lasts),
        in_specs=smem(3) + vmem(8),
        out_specs=vmem(1)[0],
        out_shape=jax.ShapeDtypeStruct((total, rows), F32),
        scratch_shapes=[pltpu.VMEM((span, 2 * total), F32)] * 3
        + [pltpu.VMEM((height, 4 * total), BF16) for height in (span, span - wide, rows)],
        compiler_params=PARAMS,
        cost_estimate=cost(3),
        name="sweeps",
    )(where, columns, columns_halo, a_own, a_near, residual, one, two, fwd, back, made[0][2])

    returned = deal(result.reshape(n_tm, steps, rows))
    return iterate + returned.transpose(1, 0, 2).reshape(steps, rows_dev)


def solution(mesh):
    placed = (
        P("space"),
        P("tm", "space"),
        P("tm", "space"),
        P("space", None, None),
        P("space", None),
        P("space"),
    )
    return jax.shard_map(local, mesh=mesh, in_specs=placed, out_specs=P("tm", "space"), check_vma=False)
```

```python
import functools
import math

import jax
import jax.numpy as jnp
import numpy as np
from jax import lax
from jax.experimental import pallas as pl
from jax.experimental.pallas import tpu as pltpu
from jax.sharding import PartitionSpec as P

GHOST = 4
CORNER_WEIGHT = 0.05
AXES = ("tm", "space")
F32 = jnp.float32
BF16 = jnp.bfloat16


def there_and_back(count):
    return list(range(0, count, 2)) + list(range(count - 1 - count % 2, 0, -2))


def split(value):
    high = value.astype(BF16)
    return high, (value - high.astype(F32)).astype(BF16)


def np_split(value):
    high = value.astype(np.float32).astype(BF16)
    return high, (value - high.astype(np.float64)).astype(np.float32).astype(BF16)


def tables(total, times):
    half = total // 2
    freq = np.arange(half)
    t = np.asarray(times)[:, None]
    angle = 2.0 * math.pi * ((t * freq[None]) % total) / total
    nyquist = np.where(t % 2 == 0, 1.0, -1.0)
    cos, sin = np.cos(angle), np.sin(angle)
    grow = CORNER_WEIGHT ** (t / total)

    def swapped(value):
        return np.roll(value, half, axis=1)

    forward = np.concatenate([cos, nyquist, -sin[:, 1:]], axis=1) * grow
    high, low = np_split(np.concatenate([forward, swapped(forward)], axis=1))
    forward = np.concatenate([high, low], axis=1)
    twice = np.where(freq == 0, 1.0, 2.0)[None]
    high, low = np_split(np.concatenate([twice * cos, nyquist, -2.0 * sin[:, 1:]], axis=1) / grow / total)
    back = np.concatenate([high, swapped(low)] * 2, axis=1)
    root = CORNER_WEIGHT ** (1.0 / total)
    theta = 2.0 * math.pi * freq / total
    lam_re = np.concatenate([1.0 - root * np.cos(theta), [1.0 + root], 1.0 - root * np.cos(theta[1:])])
    lam_im = np.concatenate([root * np.sin(theta), [0.0], -root * np.sin(theta[1:])])
    lam = np.stack([lam_re, lam_im])
    return np.concatenate([forward] * 2, axis=0), back, np.concatenate([lam, swapped(lam)], axis=1).astype(np.float32)


def place(lower_ref, upper_ref, at, value):
    half = value.shape[1] // 2
    turned = pltpu.roll(value, half, 1)
    low = lax.broadcasted_iota(jnp.int32, value.shape, 1) < half
    for i, (first, second) in enumerate(((value, turned), (turned, value))):
        for ref, part in ((lower_ref, jnp.where(low, first, 0.0)), (upper_ref, jnp.where(low, 0.0, second))):
            ref[at + i] = jnp.concatenate(split(part), axis=0)


def couple(block, at, lower_ref, upper_ref):
    size, width = block.shape
    tiles = [lower_ref[at[n]] + upper_ref[at[n + 1]] for n in range(0, len(at) - 1, 2)]
    if len(at) % 2:
        tiles.append(lower_ref[at[-1]])
    picked = jnp.concatenate(tiles, axis=1)[:, :width]
    out = lax.dot_general(
        picked, jnp.concatenate(split(block), axis=0), (((1,), (1,)), ((), ())), preferred_element_type=F32
    )
    steps = out.shape[0] // 2
    out = out[:steps] + out[steps:]
    return out + pltpu.roll(out, size, 1)


def couple_rows(blocks_ref, origin, cols_ref, base, rows, lower_ref, upper_ref, put):
    slots = cols_ref.shape[0]
    size = blocks_ref.shape[1]
    for b in rows:
        pair = [
            couple(blocks_ref[i - origin], [cols_ref[n, i] - base for n in range(slots)], lower_ref, upper_ref)
            for i in (b, b + 1)
        ]
        low = lax.broadcasted_iota(jnp.int32, pair[0].shape, 1) < size
        put(b // 2, jnp.where(low, pair[0], pair[1]))


def sides_kernel(where_ref, x_ref, blocks_ref, one_ref, two_ref):
    even = where_ref[6] == 1
    extent = one_ref.shape[1]
    low, high = x_ref[:, :extent], x_ref[:, x_ref.shape[1] - extent :]
    one_ref[...] = jnp.where(even, high, low)
    two_ref[...] = jnp.where(even, low, high)


def inner_kernel(where_ref, cols_ref, x_ref, blocks_ref, out_ref, lower_ref, upper_ref):
    block_rows = blocks_ref.shape[0]

    def put(i, value):
        out_ref[:, i * 128 : (i + 1) * 128] = value

    for b in range(0, block_rows, 2):
        place(lower_ref, upper_ref, b, x_ref[:, b * 64 : b * 64 + 128])
    rows = range(GHOST, block_rows - GHOST, 2)
    couple_rows(blocks_ref, 0, cols_ref, where_ref[5], rows, lower_ref, upper_ref, put)


def outer_kernel(
    where_ref, cols_ref, x_ref, f_ref, blocks_ref, inner_ref, two_ref, one_ref, start_ref, kd_ref, out_ref, rim_ref,
    lower_ref, upper_ref, edge_ref,
):
    block_rows = cols_ref.shape[1]
    steps = x_ref.shape[0]
    peers, height, _ = out_ref.shape
    tall = x_ref.shape[1] // peers // 128
    even, opening = where_ref[6] == 1, where_ref[7] == 1
    for i in range(0, GHOST, 2):
        lanes = slice(i * 64, i * 64 + 128)
        first, second = one_ref[:, lanes], two_ref[:, lanes]
        place(lower_ref, upper_ref, i, jnp.where(even, second, first))
        place(lower_ref, upper_ref, GHOST + block_rows + i, jnp.where(even, first, second))
    ends = list(range(0, 2 * GHOST, 2)) + list(range(block_rows - 2 * GHOST, block_rows, 2))
    for b in ends:
        place(lower_ref, upper_ref, GHOST + b, x_ref[:, b * 64 : b * 64 + 128])

    def put(i, value):
        edge_ref[i] = value

    outer = [b for b in ends if b < GHOST or b >= block_rows - GHOST]
    couple_rows(blocks_ref, 0, cols_ref, where_ref[5] - GHOST, outer, lower_ref, upper_ref, put)
    for i in range(x_ref.shape[1] // 128):
        lanes = slice(i * 128, (i + 1) * 128)
        now = x_ref[:, lanes]
        coupled = edge_ref[i] if 2 * i in outer else inner_ref[:, lanes]
        kd = kd_ref[i : i + 1, :]
        before = jnp.where(opening, start_ref[i : i + 1, :], 0.0)
        previous = jnp.concatenate([before, now[: steps - 1]], axis=0)
        p, j = i // tall, i % tall
        out_ref[p, j * steps : (j + 1) * steps, :] = f_ref[:, lanes] + previous - (1.0 + kd) * now - coupled
        out_ref[p, steps * tall + j : steps * tall + j + 1, :] = now[steps - 1 :]
        out_ref[p, (steps + 1) * tall + j : (steps + 1) * tall + j + 1, :] = kd
    used = (steps + 2) * tall
    if used < height:
        out_ref[:, used:, :] = jnp.zeros((peers, height - used, 128), F32)

    lowest = where_ref[0] == 0
    _, size, width = blocks_ref.shape
    slots = width // size
    lane = lax.broadcasted_iota(jnp.int32, (8, width), 1)
    found = jnp.zeros((8, width), jnp.int32)
    for b in range(GHOST):
        last = block_rows - GHOST + b
        rim_ref[b * size : (b + 1) * size, :] = jnp.where(lowest, blocks_ref[b], blocks_ref[last])
        for n in range(slots):
            found = jnp.where(lane == n * GHOST + b, cols_ref[n, jnp.where(lowest, b, last)], found)
    rim_ref[GHOST * size :, :] = found.astype(F32)


def blocks_kernel(where_ref, blocks_ref, rim_ref, own_ref, near_ref, buffer, sems):
    count, size, _ = buffer.shape
    chunk = count - 2 * GHOST
    block_rows = blocks_ref.shape[0]
    spot = where_ref[0]
    own = list(range(GHOST, GHOST + chunk))
    others = list(range(GHOST)) + list(range(GHOST + chunk, count))
    mine = blocks_ref.at[pl.ds(spot * chunk, chunk)]
    copies = {GHOST: pltpu.make_async_copy(mine, buffer.at[pl.ds(GHOST, chunk)], sems.at[GHOST])}
    for b in others:
        row = jnp.clip(spot * chunk + b - GHOST, 0, block_rows - 1)
        copies[b] = pltpu.make_async_copy(blocks_ref.at[row], buffer.at[b], sems.at[b])
    for copy in copies.values():
        copy.start()
    for b in own + others:
        if b in copies:
            copies[b].wait()
        value = buffer[b]
        if GHOST <= b < GHOST + chunk:
            ref, at = own_ref, b - GHOST
        else:
            ref, at = near_ref, b if b < GHOST else b - chunk
            row = spot * chunk + b - GHOST
            if rim_ref.shape[0] > GHOST * size + 8:
                at_rim = jnp.where(row < 0, row + GHOST, GHOST + row - block_rows)
            else:
                at_rim = jnp.where(row < 0, row + GHOST, row - block_rows)
            outside = (row < 0) | (row >= block_rows)
            at_rim = pl.multiple_of(jnp.where(outside, at_rim, 0) * size, size)
            value = jnp.where(outside, rim_ref[pl.ds(at_rim, size), :], value)
        high, low = split(value)
        ref[at, :size] = high
        ref[at, size:] = low


def product(a, at, v_ref, size):
    picked = jnp.concatenate([v_ref[pl.ds(pl.multiple_of(row, size), size), :] for row in at], axis=0)
    out = jnp.dot(a, picked, preferred_element_type=F32)
    out = out[:size] + out[size:]
    half = out.shape[1] // 2
    return out[:, :half] + out[:, half:]


def store_split(ref, at, value):
    high, low = split(value)
    rows, channels = value.shape
    half = ref.shape[1] // 2
    ref[at : at + rows, :channels] = high
    ref[at : at + rows, half : half + channels] = low


def gather_chunk(pick, crossed, flip, lasts, dims):
    size, slots, chunk, total, steps = dims
    tall = chunk * size // 128
    count = total // steps
    parts = []
    for j in range(count):
        last = jnp.where(flip == 1, lasts[1][j], lasts[0][j])
        at = jnp.maximum(last, 0)
        held = pick(jnp.where(crossed, count - 1 - j, j))
        other = pick(jnp.where(crossed, count - 1 - at, at))
        wide = [held[i * steps : (i + 1) * steps] for i in range(tall)]
        before = [other[steps * tall + i : steps * tall + i + 1] for i in range(tall)]
        wide, before = jnp.concatenate(wide, axis=1), jnp.concatenate(before, axis=1)
        opens = lax.broadcasted_iota(jnp.int32, wide.shape, 0) == 0
        parts.append(wide + jnp.where(opens & (last >= 0), before, 0.0))
    kd = jnp.concatenate([held[(steps + 1) * tall + i : (steps + 1) * tall + i + 1] for i in range(tall)], axis=1)
    return jnp.concatenate(parts, axis=0), kd


def sweeps_kernel(
    dims, lasts, where_ref, cols_ref, near_ref, a_ref, an_ref, r_ref, one_ref, two_ref, fwd_ref, back_ref, lam_ref, out_ref,
    s_ref, cr_ref, ci_ref, v0_ref, v1_ref, y_ref,
):
    size, slots, chunk, total, steps = dims
    rows = chunk * size
    wide = 2 * GHOST * size
    spot, flip, base, even = where_ref[0], where_ref[1], where_ref[2], where_ref[3] == 1
    count = total // steps
    block_rows = cols_ref.shape[1]
    fwd = fwd_ref[flip]

    def forward(at, value):
        high, low = split(value)
        stacked = jnp.concatenate([high, low], axis=0)
        out = lax.dot_general(stacked, fwd, (((0,), (0,)), ((), ())), preferred_element_type=F32)
        s_ref[at : at + value.shape[1], :] = out[:, : 2 * total] + out[:, 2 * total :]

    def near(first_ref, second_ref, hop):
        return lambda at: jnp.where(even, second_ref[hop, at], first_ref[hop, at])

    hops = one_ref.shape[0]
    chunks = [(near(one_ref, two_ref, h), spot < hops - h) for h in range(hops)]
    chunks += [(lambda at: r_ref[at], False)]
    chunks += [(near(two_ref, one_ref, h), spot >= count - 1 - h) for h in range(hops)]
    kds = []
    for i, (pick, crossed) in enumerate(chunks):
        residual, kd = gather_chunk(pick, crossed, flip, lasts, dims)
        forward(i * rows, residual)
        kds.append(kd)
    kd = jnp.concatenate(kds, axis=1)
    kd = jnp.broadcast_to(kd, (2 * total, kd.shape[1])).T
    diag = kd + lam_ref[0:1, :]
    imag = lam_ref[1:2, :]
    inverse = 1.0 / (diag * diag + imag * imag)
    cr_ref[...] = diag * inverse
    ci_ref[...] = imag * inverse

    def divide(value, at):
        span = slice(at, at + value.shape[0])
        return value * cr_ref[span, :] + pltpu.roll(value, total, 1) * ci_ref[span, :]

    def column(n, b):
        row = spot * chunk + b
        if 0 <= b < chunk:
            return cols_ref[n, row] - base
        found = cols_ref[n, jnp.clip(row, 0, block_rows - 1)]
        if b < 0:
            found = jnp.where(row < 0, near_ref[n, jnp.clip(row + GHOST, 0, GHOST - 1)], found)
        if b >= chunk:
            found = jnp.where(row >= block_rows, near_ref[n, GHOST + jnp.clip(row - block_rows, 0, GHOST - 1)], found)
        return jnp.clip(found - base, -2 * GHOST, chunk + 2 * GHOST - 1)

    store_split(v0_ref, 0, divide(s_ref[...], 0))
    for b in range(-GHOST, chunk + GHOST):
        at = (b + 2 * GHOST) * size
        a = a_ref[b] if 0 <= b < chunk else an_ref[b + GHOST if b < 0 else b - chunk + GHOST]
        coupled = product(a, [(column(n, b) + 2 * GHOST) * size for n in range(slots)], v0_ref, size)
        store_split(v1_ref, at - GHOST * size, divide(s_ref[at : at + size, :] - coupled, at))
    for b in range(chunk):
        at = (b + 2 * GHOST) * size
        coupled = product(a_ref[b], [(column(n, b) + GHOST) * size for n in range(slots)], v1_ref, size)
        store_split(y_ref, b * size, divide(s_ref[at : at + size, :] - coupled, at))
    change = lax.dot_general(back_ref[flip], y_ref[...], (((1,), (1,)), ((), ())), preferred_element_type=F32)
    out_ref[...] = change


def vmem(count):
    return [pl.BlockSpec(memory_space=pltpu.VMEM)] * count


def smem(count):
    return [pl.BlockSpec(memory_space=pltpu.SMEM)] * count


def cost(microseconds):
    return pl.CostEstimate(flops=0, transcendentals=0, bytes_accessed=3_000_000 * microseconds)


PARAMS = pltpu.CompilerParams(vmem_limit_bytes=16 * 1024 * 1024)
BLOCKS_PARAMS = pltpu.CompilerParams(vmem_limit_bytes=48 * 1024 * 1024)


def local(start_state, forcing, iterate, blocks, columns, kdiag):
    steps, rows_dev = iterate.shape
    block_rows, size, width = blocks.shape
    slots = width // size
    n_tm, n_space = lax.axis_size("tm"), lax.axis_size("space")
    total = steps * n_tm
    chunk = block_rows // n_tm
    rows = chunk * size
    edge = GHOST * size
    wide = 2 * edge
    dims = (size, slots, chunk, total, steps)
    order = there_and_back(n_tm)

    tm_index, space_index = lax.axis_index("tm"), lax.axis_index("space")
    flipped = space_index % 2 == 1
    spot = jnp.where(tm_index % 2 == 0, tm_index // 2, n_tm - 1 - tm_index // 2)
    spot = jnp.where(flipped, n_tm - 1 - spot, spot)
    even = (space_index * n_tm + spot) % 2 == 0

    groups, ring = [], []
    for s in range(n_space):
        members = [t * n_space + s for t in (order if s % 2 == 0 else order[::-1])]
        groups.append(tuple(members))
        ring += members
    groups = tuple(groups)
    count = len(ring)

    def deal(value):
        return lax.all_to_all(value, AXES, 0, 0, axis_index_groups=groups, tiled=True)

    def ring_pairs(first):
        pairs = []
        for i in range(first, count - 1, 2):
            pairs += [(ring[i], ring[i + 1]), (ring[i + 1], ring[i])]
        return pairs

    def neighbours(value, hops):
        if hops == 1:
            return [lax.ppermute(value, AXES, ring_pairs(first))[None] for first in (0, 1)]
        left, right = [], []
        for hop in range(1, hops + 1):
            up = [(ring[i], ring[i + hop]) for i in range(count - hop)]
            left.insert(0, lax.ppermute(value, AXES, up))
            right.append(lax.ppermute(value, AXES, [(j, i) for i, j in up]))
        return jnp.stack(left), jnp.stack(right)

    times = [[t * steps + j for t in members for j in range(steps)] for members in (order, order[::-1])]
    made = [tables(total, at) for at in times]
    fwd = np.stack([made[0][0], made[1][0]])
    back = np.stack([made[0][1], made[1][1]])
    lasts = [[at.index(at[j] - 1) // steps if at[j] else -1 for j in range(0, total, steps)] for at in times]
    base = space_index * block_rows + spot * chunk
    hops = wide // rows
    here = [spot, flipped, base, even & (hops == 1), spot, space_index * block_rows, space_index % 2 == 0, tm_index == 0]
    where = jnp.stack([jnp.asarray(value, jnp.int32) for value in here])
    columns = columns.T

    given = pl.pallas_call(
        sides_kernel,
        in_specs=smem(1) + vmem(1) + [pl.BlockSpec(memory_space=pl.ANY)],
        out_specs=vmem(2),
        out_shape=[jax.ShapeDtypeStruct((steps, edge), F32)] * 2,
        compiler_params=BLOCKS_PARAMS,
        name="sides",
    )(where, iterate, blocks)
    sides = []
    for first in (1, 0):
        pairs = [(s, s + 1) for s in range(first, n_space - 1, 2)]
        sides.insert(0, lax.ppermute(given[first], "space", pairs + [(j, i) for i, j in pairs]))
    inner = pl.pallas_call(
        inner_kernel,
        in_specs=smem(2) + vmem(2),
        out_specs=vmem(1)[0],
        out_shape=jax.ShapeDtypeStruct((steps, rows_dev), F32),
        scratch_shapes=[pltpu.VMEM((block_rows, 2 * steps, 2 * size), BF16)] * 2,
        compiler_params=PARAMS,
        name="inner",
    )(where, columns, iterate, blocks)
    tall = rows // 128
    height = -(-(steps + 2) * tall // 8) * 8
    residual, rim = pl.pallas_call(
        outer_kernel,
        in_specs=smem(2) + vmem(8),
        out_specs=vmem(2),
        out_shape=[
            jax.ShapeDtypeStruct((n_tm, height, 128), F32),
            jax.ShapeDtypeStruct((edge + 8, width), F32),
        ],
        scratch_shapes=[pltpu.VMEM((block_rows + 2 * GHOST, 2 * steps, 2 * size), BF16)] * 2
        + [pltpu.VMEM((block_rows // 2, steps, 128), F32)],
        compiler_params=PARAMS,
        cost_estimate=cost(1),
        name="outer",
    )(where, columns, iterate, forcing, blocks, inner, *sides[::-1], start_state.reshape(-1, 128), kdiag.reshape(-1, 128))
    residual = deal(residual)

    def rim_columns(value):
        return value[edge, : GHOST * slots].reshape(slots, GHOST).astype(jnp.int32)

    if chunk >= 2 * GHOST and n_tm > 1:
        pairs = []
        for s in range(n_space - 1):
            i, j = ring[(s + 1) * n_tm - 1], ring[(s + 1) * n_tm]
            pairs += [(i, j), (j, i)]
        rim = lax.ppermute(rim, AXES, pairs)
        columns_halo = jnp.concatenate([rim_columns(rim)] * 2, axis=1)
    else:
        up = [(s, s + 1) for s in range(n_space - 1)]
        down = [(j, i) for i, j in up]
        rim = [
            lax.ppermute(value, "space", pairs)
            for value, pairs in ((blocks[-GHOST:], up), (columns[:, -GHOST:], up), (blocks[:GHOST], down), (columns[:, :GHOST], down))
        ]
        columns_halo = jnp.concatenate(rim[1::2], axis=1)
        rim = jnp.concatenate([value.reshape(edge, width) for value in rim[::2]], axis=0)
    a_own, a_near = pl.pallas_call(
        blocks_kernel,
        in_specs=smem(1) + [pl.BlockSpec(memory_space=pl.ANY)] + vmem(1),
        out_specs=vmem(2),
        out_shape=[jax.ShapeDtypeStruct((n, 2 * size, width), BF16) for n in (chunk, 2 * GHOST)],
        scratch_shapes=[
            pltpu.VMEM((chunk + 2 * GHOST, size, width), F32),
            pltpu.SemaphoreType.DMA((chunk + 2 * GHOST,)),
        ],
        compiler_params=BLOCKS_PARAMS,
        cost_estimate=cost(2),
        name="blocks",
    )(where, blocks, rim)

    one, two = neighbours(residual, hops)
    span = rows + 2 * wide
    result = pl.pallas_call(
        functools.partial(sweeps_kernel, dims, lasts),
        in_specs=smem(3) + vmem(8),
        out_specs=vmem(1)[0],
        out_shape=jax.ShapeDtypeStruct((total, rows), F32),
        scratch_shapes=[pltpu.VMEM((span, 2 * total), F32)] * 3
        + [pltpu.VMEM((height, 4 * total), BF16) for height in (span, span - wide, rows)],
        compiler_params=PARAMS,
        cost_estimate=cost(3),
        name="sweeps",
    )(where, columns, columns_halo, a_own, a_near, residual, one, two, fwd, back, made[0][2])

    returned = deal(result.reshape(n_tm, steps, rows))
    return iterate + returned.transpose(1, 0, 2).reshape(steps, rows_dev)


def solution(mesh):
    placed = (
        P("space"),
        P("tm", "space"),
        P("tm", "space"),
        P("space", None, None),
        P("space", None),
        P("space"),
    )
    return jax.shard_map(local, mesh=mesh, in_specs=placed, out_specs=P("tm", "space"), check_vma=False)
```
